256 devices in a mesh: rows: 256 (over y, x, z, core).
Axes of the slice: x: 4, y: 4, z: 8, core: 2. Of those that a mesh axis runs over, the one named last changes fastest.
Arguments:
- embed: float32 [1048576, 64], P('rows'), may hold values from -6 to 6
- amplitude: float32 [1048576], P('rows'), may hold values from 0.4 to 4.3, as said below
- pivots: int32 [4, 128], replicated, may hold values from 0 to 1048575, as said below
Outputs:
- factor: float32 [1048576, 512], P('rows')
- residual: float32 [1048576], P('rows')
- means: float32 [4], replicated
The draws below stay inside these ranges and needn't reach their ends.
Inputs may be any that keep to these rules, and one draw needn't show every extreme that they name: `pivots`: global point ids; all 512 ids are distinct. Within one panel at most 2 ids lie on one device (a block of 4096 consecutive ids), and in every panel some device holds exactly 2. `amplitude`: Positive.
All inputs are finite; a program needn't handle non-finite values.
Results may differ from the reference program's by a relative error of at most 0.0003.
Values sent between devices are 32-bit elements; how exact they have to be, the bound alone decides.
A program may use at most 128 MiB of HBM per device.

```python
import jax
import jax.numpy as jnp
from jax import lax

EMB = 64
PB = 128
PANELS = 4
ROWS_DEV = 4096
NPTS = 1048576
CAP = 2


def draw_amplitude(key, part):
    key = jax.random.fold_in(key, 3)
    place = jnp.arange(NPTS, dtype=jnp.float32) / NPTS
    noise = jax.random.uniform(key, (NPTS,), jnp.float32, -0.5, 0.5)
    return jnp.exp(noise + 0.55 * place)


def draw_pivots(key, part):
    key = jax.random.fold_in(key, 7)
    owners_all = NPTS // ROWS_DEV
    total_slots = owners_all * CAP
    slot_ids = jnp.arange(total_slots, dtype=jnp.int32)
    slot_owner = slot_ids // CAP
    slot_place = slot_ids % CAP
    panels = []
    for panel in range(PANELS):
        panel_key = jax.random.fold_in(key, panel)
        key_full, key_order, key_mix, key_spot = jax.random.split(panel_key, 4)
        full_owner = jax.random.randint(key_full, (), 0, owners_all, dtype=jnp.int32)
        ranking = jax.random.permutation(key_order, total_slots).astype(jnp.int32)
        score = jnp.where(slot_owner == full_owner, slot_place - CAP, ranking)
        picked = jnp.argsort(score, stable=True)[:PB].astype(jnp.int32)
        picked = picked[jax.random.permutation(key_mix, PB)]
        owner = picked // CAP
        place = picked % CAP
        spread = jax.random.randint(key_spot, (PB,), 0, ROWS_DEV // (PANELS * CAP), dtype=jnp.int32)
        local = panel * CAP + place + PANELS * CAP * spread
        panels.append(owner * ROWS_DEV + local)
    return jnp.stack(panels).astype(jnp.int32)


def level_of(rng, dims, cuts, low, high):
    gain, own = 1.0, jax.random.fold_in(rng, 6)
    for axis_at, parts in cuts:
        steps = jnp.exp(jax.random.uniform(jax.random.fold_in(own, axis_at), (parts,), jnp.float32, low / len(cuts), high / len(cuts)))
        gain = gain * jnp.repeat(steps, dims[axis_at] // parts).reshape([-1 if axis == axis_at else 1 for axis in range(len(dims))])
    return gain


def scatter_about(rng, shape, deviation, reach, cuts=(), held_as=jnp.bfloat16):
    array = deviation * jax.random.normal(rng, shape, jnp.float32)
    if cuts:
        array = array * level_of(rng, shape, cuts, -0.22, 0.18)
    return jnp.clip(array, -reach, reach).astype(held_as)


def setup_inputs(seed: int = 0) -> dict:
    seeds = jax.random.split(jax.random.key(seed), 4)
    return {
        "embed": scatter_about(seeds[0], (NPTS, EMB), 1.0, 6.0, ((0, 256),), jnp.float32),
        "amplitude": draw_amplitude(jax.random.fold_in(seeds[3], 71), 0),
        "pivots": draw_pivots(jax.random.fold_in(seeds[3], 71), 0),
    }


def kernel_block(left, left_amp, left_sq, right, right_amp, right_sq):
    inner = jnp.dot(left.astype(jnp.float32), right.T.astype(jnp.float32), precision=lax.Precision.HIGHEST, preferred_element_type=jnp.float32)
    dist = jnp.maximum(left_sq[:, None] + right_sq[None, :] - 2.0 * inner, 0.0)
    return left_amp[:, None] * right_amp[None, :] * jnp.exp(-dist / EMB)

def lower_inverse(block):
    lower = jnp.linalg.cholesky(0.5 * (block + block.T))
    ident = jnp.eye(block.shape[0], dtype=block.dtype)
    return lax.linalg.triangular_solve(lower, ident, left_side=True, lower=True)

def reference(embed, amplitude, pivots):
    squared = jnp.sum(embed * embed, axis=1)
    residual = amplitude * amplitude
    columns = []
    means = []
    for panel in range(PANELS):
        pivot_ids = pivots[panel]
        chosen = embed[pivot_ids]
        chosen_amp = amplitude[pivot_ids]
        chosen_sq = jnp.sum(chosen * chosen, axis=1)
        cross = kernel_block(embed, amplitude, squared, chosen, chosen_amp, chosen_sq)
        block = kernel_block(chosen, chosen_amp, chosen_sq, chosen, chosen_amp, chosen_sq)
        if columns:
            factor = jnp.concatenate(columns, axis=1)
            chosen_rows = factor[pivot_ids]
            cross = cross - jnp.dot(factor.astype(jnp.float32), chosen_rows.T.astype(jnp.float32), precision=lax.Precision.HIGHEST, preferred_element_type=jnp.float32)
            block = block - jnp.dot(chosen_rows.astype(jnp.float32), chosen_rows.T.astype(jnp.float32), precision=lax.Precision.HIGHEST, preferred_element_type=jnp.float32)
        inverse = lower_inverse(block)
        fresh = jnp.dot(cross.astype(jnp.float32), inverse.T.astype(jnp.float32), precision=lax.Precision.HIGHEST, preferred_element_type=jnp.float32)
        columns.append(fresh)
        residual = residual - jnp.sum(fresh * fresh, axis=1)
        means.append(jnp.mean(residual))
    return (jnp.concatenate(columns, axis=1), residual, jnp.stack(means))
```

```python
import functools

import jax
import jax.numpy as jnp
from jax import lax
from jax.experimental import pallas as pl
from jax.experimental.pallas import tpu as pltpu
from jax.sharding import PartitionSpec as P
HI = lax.Precision.HIGHEST
F32 = jnp.float32

def spread_row(block, row):
    return jnp.broadcast_to(block[row:row+1, :], (8, 128))

def spread_col(block, col):
    return jnp.broadcast_to(block[:, col:col+1], (8, 128))

def eliminate(blocks, lookahead=True):
    lane = lax.broadcasted_iota(jnp.int32, (8, 128), 1)
    sub = lax.broadcasted_iota(jnp.int32, (8, 128), 0)
    n = len(blocks)
    blocks = list(blocks)
    diag = [spread_col(blocks[0], k) for k in range(8)]
    for j in range(n):
        inside = (lane >= 8 * j) & (lane < 8 * j + 8)
        below = {b: [spread_col(blocks[b], 8 * j + k) for k in range(8)] for b in range(j + 1, n)}
        nxt = [spread_col(blocks[j + 1], 8 * (j + 1) + k) for k in range(8)] if j + 1 < n else None
        rest = jnp.where(inside, jnp.where(lane - 8 * j == sub, 1.0, 0.0), blocks[j])
        rows = []
        for k in range(8):
            scale = lax.rsqrt(spread_row(diag[k], k))
            low = diag[k] * scale
            row = spread_row(rest, k) * scale
            rows.append(row)
            if k < 7:
                rest = rest - low * row
            for b in below:
                below[b][k] = below[b][k] * scale
            for m in range(k + 1, 8):
                factor = spread_row(low, m)
                diag[m] = diag[m] - low * factor
                for b in below:
                    below[b][m] = below[b][m] - below[b][k] * factor
        out = rows[0]
        for k in range(1, 8):
            out = jnp.where(sub == k, rows[k], out)
        blocks[j] = out
        if j + 1 < n:
            w = below[j + 1]
            for k in range(8):
                t = [w[l] * spread_row(w[l], k) for l in range(8)]
                t = ((t[0] + t[1]) + (t[2] + t[3])) + ((t[4] + t[5]) + (t[6] + t[7]))
                nxt[k] = nxt[k] - t
            diag = nxt
        for b in below:
            t = [below[b][l] * rows[l] for l in range(8)]
            t = ((t[0] + t[1]) + (t[2] + t[3])) + ((t[4] + t[5]) + (t[6] + t[7]))
            blocks[b] = jnp.where(inside, 0.0, blocks[b]) - t
    return blocks

def lower_inverse_512(a_ref, store):
    lane = lax.broadcasted_iota(jnp.int32, (128, 128), 1)
    sub = lax.broadcasted_iota(jnp.int32, (128, 128), 0)
    size = a_ref.shape[0]
    panels = size // 128
    for p in range(panels):
        lo = 128 * p
        got = eliminate([a_ref[lo + 8 * b: lo + 8 * b + 8, lo:lo + 128] for b in range(16)])
        inv = jnp.where(lane <= sub, jnp.concatenate(got, axis=0), 0.0)
        right = None
        if p + 1 < panels:
            right = jnp.dot(inv, a_ref[lo:lo + 128, lo + 128:], precision=HI, preferred_element_type=F32)
            a_ref[lo + 128:, lo + 128:] -= lax.dot_general(right, right, (((0,), (0,)), ((), ())), precision=HI, preferred_element_type=F32)
        left = inv
        if p:
            left = jnp.concatenate([jnp.dot(inv, a_ref[lo:lo + 128, :lo], precision=HI, preferred_element_type=F32), inv], axis=1)
        store(p, left)
        if p + 1 < panels:
            upd = lax.dot_general(right, left, (((0,), (0,)), ((), ())), precision=HI, preferred_element_type=F32)
            if p:
                a_ref[lo + 128:, :lo] -= upd[:, :lo]
            a_ref[lo + 128:, lo:lo + 128] = -upd[:, lo:]

LOG2E = 1.4426950408889634
MESH = pl.DeviceIdType.MESH
BF16 = jnp.bfloat16


def split_two(value):
    high = value.astype(BF16)
    return high, (value - high.astype(F32)).astype(BF16)


def split_three(value):
    high = value.astype(BF16)
    left = value - high.astype(F32)
    middle = left.astype(BF16)
    return high, middle, (left - middle.astype(F32)).astype(BF16)


def place():
    me = lax.axis_index("rows")
    core = lax.rem(me, 2)
    deep = lax.rem(me // 2, 8)
    plane = me // 16
    return me, core, deep, plane


def device_of(plane, deep, core):
    return (plane * 8 + deep) * 2 + core


def features_of(embed_ref, amp_ref, first):
    part = embed_ref[:, first:first + 128]
    amp = amp_ref[first // 128:first // 128 + 1, :]
    squared = jnp.sum(part * part, axis=0, keepdims=True) * (LOG2E / 64)
    high, low = split_two(part)
    high, low = high.astype(F32), low.astype(F32)
    ones = jnp.ones((1, 128), F32)
    extra = [v.astype(F32) for v in split_three(squared)] + [ones] * 3 + [v.astype(F32) for v in split_three(amp)]
    row = lax.broadcasted_iota(jnp.int32, (64, 128), 0)
    tail = jnp.zeros((64, 128), F32)
    for index, value in enumerate(extra):
        tail = jnp.where(row == index, value, tail)
    one = jnp.concatenate([high, low], axis=0).T.astype(BF16)
    two = jnp.concatenate([high, tail], axis=0).T.astype(BF16)
    return one, two


def gather_kernel(pivots_ref, embed_ref, amp_ref, features_ref, chosen_ref,
                  own, column, whole, send1, recv1, send2, recv2, send3, recv3):
    me, core, deep, plane = place()
    barrier = pltpu.get_barrier_semaphore()
    peers1 = [device_of(plane, lax.rem(deep + d, 8), core) for d in range(1, 8)]
    peers2 = [device_of(lax.rem(plane + d, 16), deep, core) for d in range(1, 16)]
    other = device_of(plane, deep, 1 - core)
    for peer in peers1 + peers2 + [other]:
        pl.semaphore_signal(barrier, inc=1, device_id=(peer,), device_id_type=MESH)

    lane = lax.broadcasted_iota(jnp.int32, (4, 128), 1)
    pivots = pivots_ref[...]
    owners = pivots >> 12
    offsets = pivots & 4095
    mine = owners == me
    key = lane * 4096 + offsets
    first = jnp.min(jnp.where(mine, key, 128 * 4096 - 1), axis=1, keepdims=True) & 4095
    last = jnp.max(jnp.where(mine, key, 0), axis=1, keepdims=True) & 4095
    lanes = lax.broadcasted_iota(jnp.int32, (64, 128), 1)
    lanes2 = lax.broadcasted_iota(jnp.int32, (128, 128), 1)
    packed = jnp.zeros((128, 128), F32)
    for p in range(4):
        halves = []
        for found in (first, last):
            offset = jnp.broadcast_to(found[p:p + 1, 0:1], (64, 128))
            group = offset >> 7
            part = embed_ref[:, 0:128]
            for b in range(1, 32):
                part = jnp.where(group == b, embed_ref[:, 128 * b:128 * b + 128], part)
            halves.append(jnp.sum(jnp.where(lanes == (offset & 127), part, 0.0), axis=1, keepdims=True))
        packed = jnp.where(lanes2 == p, jnp.concatenate(halves, axis=0), packed)
    tile = packed.T[0:4, :]
    own[...] = tile
    column[deep] = tile

    pl.semaphore_wait(barrier, 23)

    copies1 = []
    for d in range(1, 8):
        copy = pltpu.make_async_remote_copy(
            src_ref=own, dst_ref=column.at[deep], send_sem=send1.at[d - 1], recv_sem=recv1.at[deep],
            device_id=(peers1[d - 1],), device_id_type=MESH)
        copy.start()
        copies1.append(copy)

    wanted = []
    sub2 = lax.broadcasted_iota(jnp.int32, (128, 128), 0)
    for p in range(4):
        row = jnp.broadcast_to(owners[p:p + 1, :], (128, 128)).astype(F32)
        col = row.T
        slot = jnp.sum(jnp.where((row == col) & (lanes2 < sub2), 1.0, 0.0), axis=1, keepdims=True)
        owner = col.astype(jnp.int32)
        spot = (owner & 1) * 128 + (owner >> 1)
        wanted.append((spot, slot))

    for start in range(0, 1024, 128):
        one, two = features_of(embed_ref, amp_ref, start)
        features_ref[start:start + 128, 0:128] = one
        features_ref[start:start + 128, 128:256] = two

    for d in range(1, 8):
        source = lax.rem(deep + d, 8)
        pltpu.make_async_remote_copy(
            src_ref=own, dst_ref=column.at[source], send_sem=send1.at[d - 1], recv_sem=recv1.at[source],
            device_id=(peers1[d - 1],), device_id_type=MESH).wait_recv()
    block = core * 16 + plane
    for p in range(4):
        whole[p, block] = jnp.concatenate([column[z][p:p + 1, :] for z in range(8)], axis=0)

    copies2 = []
    for d in range(1, 16):
        copy = pltpu.make_async_remote_copy(
            src_ref=whole.at[:, block], dst_ref=whole.at[:, block], send_sem=send2.at[d - 1], recv_sem=recv2.at[plane],
            device_id=(peers2[d - 1],), device_id_type=MESH)
        copy.start()
        copies2.append(copy)

    def forward(index, of_plane):
        at = core * 16 + of_plane
        copy = pltpu.make_async_remote_copy(
            src_ref=whole.at[:, at], dst_ref=whole.at[:, at], send_sem=send3.at[index], recv_sem=recv3.at[of_plane],
            device_id=(other,), device_id_type=MESH)
        copy.start()
        return copy

    copies3 = [forward(0, plane)]
    for start in range(1024, 4096, 128):
        one, two = features_of(embed_ref, amp_ref, start)
        features_ref[start:start + 128, 0:128] = one
        features_ref[start:start + 128, 128:256] = two

    for d in range(1, 16):
        source = lax.rem(plane + d, 16)
        at = core * 16 + source
        pltpu.make_async_remote_copy(
            src_ref=whole.at[:, at], dst_ref=whole.at[:, at], send_sem=send2.at[d - 1], recv_sem=recv2.at[source],
            device_id=(peers2[d - 1],), device_id_type=MESH).wait_recv()
        copies3.append(forward(d, source))
    for source in range(16):
        at = (1 - core) * 16 + source
        pltpu.make_async_remote_copy(
            src_ref=whole.at[:, at], dst_ref=whole.at[:, at], send_sem=send3.at[0], recv_sem=recv3.at[source],
            device_id=(other,), device_id_type=MESH).wait_recv()

    for p in range(4):
        spot, slot = wanted[p]
        rows = whole[p].reshape(256, 128)
        parts = jnp.concatenate(split_three(rows), axis=1)
        wide = lax.broadcasted_iota(jnp.int32, (128, 256), 1)
        take = jnp.where(wide == jnp.concatenate([spot, spot], axis=1), 1.0, 0.0).astype(BF16)
        got = jnp.dot(take, parts, preferred_element_type=F32)
        got = got[:, 0:128] + (got[:, 128:256] + got[:, 256:384])
        got = jnp.where(slot > 0.5, pltpu.roll(got, 64, 1), got)
        chosen_ref[128 * p:128 * p + 128, :] = jnp.where(lanes2 < 64, got, 0.0)

    for copy in copies1 + copies2 + copies3:
        copy.wait_send()


def gather(pivots, embed, amp):
    return pl.pallas_call(
        gather_kernel,
        out_shape=(jax.ShapeDtypeStruct((4096, 256), BF16), jax.ShapeDtypeStruct((512, 128), F32)),
        in_specs=[pl.BlockSpec(memory_space=pltpu.VMEM)] * 3,
        out_specs=(pl.BlockSpec(memory_space=pltpu.VMEM), pl.BlockSpec(memory_space=pltpu.VMEM)),
        scratch_shapes=[
            pltpu.VMEM((4, 128), F32), pltpu.VMEM((8, 4, 128), F32), pltpu.VMEM((4, 32, 8, 128), F32),
            pltpu.SemaphoreType.DMA((7,)), pltpu.SemaphoreType.DMA((8,)),
            pltpu.SemaphoreType.DMA((15,)), pltpu.SemaphoreType.DMA((16,)),
            pltpu.SemaphoreType.DMA((16,)), pltpu.SemaphoreType.DMA((16,)),
        ],
        compiler_params=pltpu.CompilerParams(collective_id=0, has_side_effects=True, vmem_limit_bytes=32 << 20),
        name="gather_pivots",
    )(pivots, embed, amp)


def product_kernel(features_ref, chosen_ref, amp_ref, factor_ref, residual_ref, sums_ref,
                   matrix, pivots_t, right0, right1, right2, right3):
    step = pl.program_id(0)
    rights = (right0, right1, right2, right3)

    @pl.when(step == 0)
    def _():
        chosen = chosen_ref[...]
        lane = lax.broadcasted_iota(jnp.int32, (512, 128), 1)
        squared = jnp.sum(chosen * chosen, axis=1, keepdims=True) * (LOG2E / 64)
        scaled = chosen * (2 * LOG2E / 64)
        left = jnp.where(lane < 64, chosen, jnp.where(lane == 64, squared, jnp.where(lane == 65, 1.0, 0.0)))
        right = jnp.where(lane < 64, scaled, jnp.where(lane == 64, -1.0, jnp.where(lane == 65, -squared, 0.0)))
        power = lax.dot_general(left, right, (((1,), (1,)), ((), ())), precision=HI, preferred_element_type=F32)
        matrix[...] = jnp.exp2(jnp.minimum(power, 0.0))
        high, low = [v.astype(F32) for v in split_two(scaled)]
        extra = [jnp.full((512, 1), -1.0, F32)] * 3 + [-v.astype(F32) for v in split_three(squared)]
        one = jnp.where(lane < 64, high, pltpu.roll(high, 64, 1))
        two = jnp.where(lane < 64, low, 0.0)
        for index, value in enumerate(extra):
            two = jnp.where(lane == 64 + index, value, two)
        pivots_t[0:128, 0:512] = one.T.astype(BF16)
        pivots_t[128:256, 0:512] = two.T.astype(BF16)
        row = lax.broadcasted_iota(jnp.int32, (256, 128), 0)
        pivots_t[:, 512:640] = jnp.where((row >= 198) & (row < 201), 1.0, 0.0).astype(BF16)

        def store(p, rows):
            for q in range(p + 1):
                high, low = split_two(rows[:, 128 * q:128 * q + 128].T)
                both = jnp.concatenate([high, low], axis=1)
                rights[p][256 * q:256 * q + 128, :] = both
                rights[p][256 * q + 128:256 * q + 256, :] = both

        lower_inverse_512(matrix, store)
        sums_ref[...] = jnp.zeros_like(sums_ref)

    power = jnp.dot(features_ref[...], pivots_t[...], preferred_element_type=F32)
    amp = power[:, 512:640]
    kern = jnp.exp2(jnp.minimum(power[:, 0:512], 0.0))
    high, low = split_two(kern)
    pieces = []
    for q in range(4):
        pieces += [high[:, 128 * q:128 * q + 128], low[:, 128 * q:128 * q + 128]]
    left = jnp.concatenate(pieces, axis=1)
    squares = jnp.zeros((256, 128), F32)
    for p in range(4):
        got = jnp.dot(left[:, :256 * (p + 1)], rights[p][...], preferred_element_type=F32)
        fresh = (got[:, 0:128] + got[:, 128:256]) * amp
        factor_ref[:, 128 * p:128 * p + 128] = fresh
        square = fresh * fresh
        squares += square
        total = square[0:8, :]
        for b in range(1, 32):
            total += square[8 * b:8 * b + 8, :]
        sums_ref[8 * p:8 * p + 8, :] += total
    both = jnp.concatenate(split_two(squares), axis=1)
    spent = lax.dot_general(jnp.ones((8, 256), BF16), both, (((1,), (1,)), ((), ())), preferred_element_type=F32)
    for b in range(2):
        own = amp_ref[pl.ds(2 * step + b, 1), :]
        residual_ref[pl.ds(2 * step + b, 1), :] = own * own - spent[0:1, 128 * b:128 * b + 128]


def product(features, chosen, amp):
    fixed = lambda i: (0, 0)
    return pl.pallas_call(
        product_kernel,
        grid=(16,),
        out_shape=(jax.ShapeDtypeStruct((4096, 512), F32), jax.ShapeDtypeStruct((32, 128), F32),
                   jax.ShapeDtypeStruct((32, 128), F32)),
        in_specs=[pl.BlockSpec((256, 256), lambda i: (i, 0)), pl.BlockSpec((512, 128), fixed),
                  pl.BlockSpec((32, 128), fixed)],
        out_specs=(pl.BlockSpec((256, 512), lambda i: (i, 0)), pl.BlockSpec((32, 128), fixed),
                   pl.BlockSpec((32, 128), fixed)),
        scratch_shapes=[pltpu.VMEM((512, 512), F32), pltpu.VMEM((256, 640), BF16)]
        + [pltpu.VMEM((256 * (p + 1), 256), BF16) for p in range(4)],
        compiler_params=pltpu.CompilerParams(vmem_limit_bytes=48 << 20),
        name="cholesky_product",
    )(features, chosen, amp)


def sums_kernel(points, sums_ref, amp_ref, means_ref, own, land1, middle, land2, send1, recv1, send2, recv2):
    me, core, deep, plane = place()
    line = deep * 2 + core
    barrier = pltpu.get_barrier_semaphore()
    peers1 = [plane * 16 + lax.rem(line + d, 16) for d in range(1, 16)]
    peers2 = [lax.rem(plane + d, 16) * 16 + line for d in range(1, 16)]
    for peer in peers1 + peers2:
        pl.semaphore_signal(barrier, inc=1, device_id=(peer,), device_id_type=MESH)

    lane = lax.broadcasted_iota(jnp.int32, (8, 128), 1)
    total = jnp.sum(amp_ref[...] * amp_ref[...])
    value = jnp.zeros((8, 128), F32)
    for p in range(4):
        total = total - jnp.sum(sums_ref[8 * p:8 * p + 8, :])
        value = jnp.where(lane == p, total, value)
    own[...] = value
    land1[line] = value
    pl.semaphore_wait(barrier, 30)

    def exchange(source, land, at, peers, send, recv):
        copies = []
        for d in range(1, 16):
            copy = pltpu.make_async_remote_copy(
                src_ref=source, dst_ref=land.at[at], send_sem=send.at[d - 1], recv_sem=recv.at[at],
                device_id=(peers[d - 1],), device_id_type=MESH)
            copy.start()
            copies.append(copy)
        for d in range(1, 16):
            origin = lax.rem(at + d, 16)
            pltpu.make_async_remote_copy(
                src_ref=source, dst_ref=land.at[origin], send_sem=send.at[d - 1], recv_sem=recv.at[origin],
                device_id=(peers[d - 1],), device_id_type=MESH).wait_recv()
        return copies, jnp.sum(land[...], axis=0)

    copies1, value = exchange(own, land1, line, peers1, send1, recv1)
    middle[...] = value
    land2[plane] = value
    copies2, value = exchange(middle, land2, plane, peers2, send2, recv2)
    means_ref[...] = value[0:1, 0:4] * (1.0 / points)
    for copy in copies1 + copies2:
        copy.wait_send()


def mean_sums(sums, amp, points):
    return pl.pallas_call(
        functools.partial(sums_kernel, points),
        out_shape=jax.ShapeDtypeStruct((1, 4), F32),
        in_specs=[pl.BlockSpec(memory_space=pltpu.VMEM)] * 2,
        out_specs=pl.BlockSpec(memory_space=pltpu.VMEM),
        scratch_shapes=[
            pltpu.VMEM((8, 128), F32), pltpu.VMEM((16, 8, 128), F32), pltpu.VMEM((8, 128), F32),
            pltpu.VMEM((16, 8, 128), F32),
            pltpu.SemaphoreType.DMA((15,)), pltpu.SemaphoreType.DMA((16,)),
            pltpu.SemaphoreType.DMA((15,)), pltpu.SemaphoreType.DMA((16,)),
        ],
        compiler_params=pltpu.CompilerParams(collective_id=1, has_side_effects=True),
        name="sum_residuals",
    )(sums, amp)


def local(embed, amplitude, pivots):
    amp = amplitude.reshape(32, 128)
    features, chosen = gather(pivots, embed.T, amp)
    factor, residual, sums = product(features, chosen, amp)
    means = mean_sums(sums, amp, 4096 * lax.axis_size("rows"))
    return factor, residual.reshape(4096), means.reshape(4)


def solution(mesh):
    return jax.shard_map(
        local,
        mesh=mesh,
        in_specs=(P("rows", None), P("rows"), P()),
        out_specs=(P("rows", None), P("rows"), P()),
        check_vma=False,
    )
```

```python
import functools

import jax
import jax.numpy as jnp
from jax import lax
from jax.experimental import pallas as pl
from jax.experimental.pallas import tpu as pltpu
from jax.sharding import PartitionSpec as P

HI = lax.Precision.HIGHEST
F32 = jnp.float32

LOG2E = 1.4426950408889634
MESH = pl.DeviceIdType.MESH
BF16 = jnp.bfloat16


def spread_row(block, row):
    return jnp.broadcast_to(block[row:row + 1, :], (8, 128))


def spread_col(block, col):
    return jnp.broadcast_to(block[:, col:col + 1], (8, 128))


def tree(terms):
    while len(terms) > 1:
        terms = [a + b for a, b in zip(terms[::2], terms[1::2])] + ([terms[-1]] if len(terms) % 2 else [])
    return terms[0]


def eliminate_rows(blocks, base, work, step):
    lane = lax.broadcasted_iota(jnp.int32, (8, 128), 1)
    sub = lax.broadcasted_iota(jnp.int32, (8, 128), 0)
    count = len(blocks)
    blocks = list(blocks)
    diag = [spread_col(blocks[0], base + k) for k in range(8)]
    for j in range(count):
        at = base + 8 * j
        inside = (lane >= at) & (lane < at + 8)
        below = {b: [spread_col(blocks[b], at + k) for k in range(8)] for b in range(j + 1, count)}
        following = [spread_col(blocks[j + 1], at + 8 + k) for k in range(8)] if j + 1 < count else None
        rest = jnp.where(inside, jnp.where(lane - at == sub, 1.0, 0.0), blocks[j])
        rows = []
        for k in range(8):
            scale = lax.rsqrt(spread_row(diag[k], k))
            low = diag[k] * scale
            row = spread_row(rest, k) * scale
            rows.append(row)
            if k < 7:
                rest = rest - low * row
            for b in below:
                below[b][k] = below[b][k] * scale
            for m in range(k + 1, 8):
                factor = spread_row(low, m)
                diag[m] = diag[m] - low * factor
                for b in below:
                    below[b][m] = below[b][m] - below[b][k] * factor
            step()
        out = rows[0]
        for k in range(1, 8):
            out = jnp.where(sub == k, rows[k], out)
        blocks[j] = out
        if j + 1 < count:
            first = below[j + 1]
            diag = [following[k] - tree([first[m] * spread_row(first[m], k) for m in range(8)]) for k in range(8)]
        for b in below:
            blocks[b] = jnp.where(inside, 0.0, blocks[b]) - tree([below[b][k] * rows[k] for k in range(8)])
        work(at // 8)
    return blocks


def eliminate(blocks, work, step, width=64):
    lane = lax.broadcasted_iota(jnp.int32, (8, 128), 1)
    blocks = list(blocks)
    group = width // 8
    for base in range(0, 128, width):
        first = base // 8
        blocks[first:first + group] = eliminate_rows(blocks[first:first + group], base, work, step)
        if base + width < 128:
            rows = jnp.concatenate(blocks[first:first + group], axis=0)
            row = lax.broadcasted_iota(jnp.int32, (width, 128), 0) + base
            col = lax.broadcasted_iota(jnp.int32, (width, 128), 1)
            lower = jnp.where((col > row) & (col < base + width), 0.0, rows)
            change = lax.dot_general(rows, lower, (((0,), (0,)), ((), ())), precision=HI, preferred_element_type=F32)
            inside = (lane >= base) & (lane < base + width)
            for b in range(first + group, 16):
                blocks[b] = jnp.where(inside, 0.0, blocks[b]) - change[8 * b:8 * b + 8, :]
    return blocks


def split_two(value):
    high = value.astype(BF16)
    return high, (value - high.astype(F32)).astype(BF16)


def split_three(value):
    high = value.astype(BF16)
    left = value - high.astype(F32)
    middle = left.astype(BF16)
    return high, middle, (left - middle.astype(F32)).astype(BF16)


def both_parts(value):
    both = jnp.concatenate(split_two(value), axis=1)
    return jnp.concatenate([both, both], axis=0)


def halves(value):
    return value[:, 0:128] + value[:, 128:256]


def prepare(chosen, matrix, pivots_t):
    lane = lax.broadcasted_iota(jnp.int32, (512, 128), 1)
    squared = jnp.sum(chosen * chosen, axis=1, keepdims=True) * (LOG2E / 64)
    scaled = chosen * (2 * LOG2E / 64)
    left = jnp.where(lane < 64, chosen, jnp.where(lane == 64, squared, jnp.where(lane == 65, 1.0, 0.0)))
    right = jnp.where(lane < 64, scaled, jnp.where(lane == 64, -1.0, jnp.where(lane == 65, -squared, 0.0)))
    power = lax.dot_general(left, right, (((1,), (1,)), ((), ())), precision=HI, preferred_element_type=F32)
    matrix[...] = jnp.exp2(jnp.minimum(power, 0.0))
    high, low = [v.astype(F32) for v in split_two(scaled)]
    extra = [jnp.full((512, 1), -1.0, F32)] * 3 + [-v.astype(F32) for v in split_three(squared)]
    one = jnp.where(lane < 64, high, pltpu.roll(high, 64, 1))
    two = jnp.where(lane < 64, low, 0.0)
    for index, value in enumerate(extra):
        two = jnp.where(lane == 64 + index, value, two)
    pivots_t[0:128, 0:512] = one.T.astype(BF16)
    pivots_t[128:256, 0:512] = two.T.astype(BF16)
    row = lax.broadcasted_iota(jnp.int32, (256, 128), 0)
    pivots_t[:, 512:640] = jnp.where((row >= 198) & (row < 201), 1.0, 0.0).astype(BF16)


CHUNK = 256
CHUNKS = 4096 // CHUNK
PIECE = 32
PER_STEP = 2


def factorise(features_ref, amp_ref, matrix, pivots_t, kern, cross, done, wide_amp, squares, inverse_t, upper,
              raw_first, raw_near, raw_far, staged, residual_ref, sent):
    sums = [[] for _ in range(4)]
    pending = []

    def step(count=PER_STEP):
        for _ in range(min(count, len(pending))):
            pending.pop(0)()

    def pieces(j):
        return [(slice(CHUNK * j + r, CHUNK * j + r + PIECE), slice(r, r + PIECE)) for r in range(0, CHUNK, PIECE)]

    def start_first(j):
        raw_first[j % 2] = jnp.dot(
            features_ref[CHUNK * j:CHUNK * j + CHUNK, :], pivots_t[...], preferred_element_type=F32)

    def end_first(j, at, part):
        wide_amp[at, :] = raw_first[j % 2, part, 512:640]
        near = jnp.exp2(jnp.minimum(raw_first[j % 2, part, 0:512], 0.0))
        cross[at, :] = jnp.concatenate(split_two(near[:, 0:128]), axis=1)
        kern[at, :] = near[:, 128:512]

    def start_near(p, j):
        raw_near[j % 2] = jnp.dot(
            cross[CHUNK * j:CHUNK * j + CHUNK, :], inverse_t[p], preferred_element_type=F32)

    def end_near(p, j, at, part):
        got = halves(raw_near[j % 2, part, :])
        fresh = got * wide_amp[at, :]
        staged[p, at, :] = fresh
        square = fresh * fresh
        sums[p].append(tree([square[8 * b:8 * b + 8, :] for b in range(PIECE // 8)]))
        if p < 3:
            squares[at, :] = square if p == 0 else squares[at, :] + square
            done[at, 256 * p:256 * p + 256] = jnp.concatenate(split_two(got), axis=1)
        else:
            squares[at, :] = squares[at, :] + square

    def start_far(p, j):
        raw_far[j % 2] = jnp.dot(
            done[CHUNK * j:CHUNK * j + CHUNK, 0:256 * (p + 1)], upper[p + 1][...], preferred_element_type=F32)

    def end_far(p, j, at, part):
        rest = kern[at, 128 * p:128 * p + 128] - halves(raw_far[j % 2, part, :])
        cross[at, :] = jnp.concatenate(split_two(rest), axis=1)

    def residual_of(j):
        both = jnp.concatenate(split_two(squares[CHUNK * j:CHUNK * j + CHUNK, :]), axis=1)
        spent = lax.dot_general(jnp.ones((8, 256), BF16), both, (((1,), (1,)), ((), ())), preferred_element_type=F32)
        for b in range(CHUNK // 128):
            row = j * (CHUNK // 128) + b
            own = amp_ref[row:row + 1, :]
            residual_ref[row:row + 1, :] = own * own - spent[0:1, 128 * b:128 * b + 128]

    def schedule(t):
        if 0 <= t < 16:
            start_first(t)
        if 1 <= t < 17:
            pending.extend(functools.partial(end_first, t - 1, *piece) for piece in pieces(t - 1))
        if 16 <= t < 80:
            start_near(t // 16 - 1, t % 16)
        if 18 <= t < 66:
            p, j = (t - 2) // 16 - 1, (t - 2) % 16
            pending.extend(functools.partial(end_far, p, j, *piece) for piece in pieces(j))
        if 17 <= t < 81:
            p, j = (t - 1) // 16 - 1, (t - 1) % 16
            pending.extend(functools.partial(end_near, p, j, *piece) for piece in pieces(j))
            pending.append(functools.partial(sent, p, j))
            if p < 3:
                pending.append(functools.partial(start_far, p, j))
        if 66 <= t < 82:
            pending.append(functools.partial(residual_of, t - 66))

    lane = lax.broadcasted_iota(jnp.int32, (128, 128), 1)
    sub = lax.broadcasted_iota(jnp.int32, (128, 128), 0)
    for p in range(4):
        lo = 128 * p

        def work(j):
            step(len(pending))
            if j < 15:
                schedule(16 * p + j + 1)

        schedule(16 * p)
        got = eliminate([matrix[lo + 8 * b:lo + 8 * b + 8, lo:lo + 128] for b in range(16)], work, step)
        inverse = jnp.where(lane <= sub, jnp.concatenate(got, axis=0), 0.0)
        inverse_t[p] = both_parts(inverse.T)
        if p < 3:
            right = jnp.dot(inverse, matrix[lo:lo + 128, lo + 128:], precision=HI, preferred_element_type=F32)
            for q in range(p + 1, 4):
                part = right[:, 128 * (q - p - 1):128 * (q - p)]
                matrix[128 * q:128 * q + 128, 128 * q:] -= lax.dot_general(
                    part, right[:, 128 * (q - p - 1):], (((0,), (0,)), ((), ())), precision=HI,
                    preferred_element_type=F32)
                upper[q][256 * p:256 * p + 256, :] = both_parts(part)
    for t in range(64, 82):
        schedule(t)
        step(len(pending))
    return [tree(parts) for parts in sums]


SCRATCH = [
    pltpu.VMEM((512, 512), F32), pltpu.VMEM((256, 640), BF16), pltpu.VMEM((4096, 384), F32),
    pltpu.VMEM((4096, 256), BF16), pltpu.VMEM((4096, 768), BF16), pltpu.VMEM((4096, 128), F32),
    pltpu.VMEM((4096, 128), F32), pltpu.VMEM((4, 256, 256), BF16),
    pltpu.VMEM((256, 256), BF16), pltpu.VMEM((512, 256), BF16), pltpu.VMEM((768, 256), BF16),
    pltpu.VMEM((2, CHUNK, 640), F32), pltpu.VMEM((2, CHUNK, 256), F32), pltpu.VMEM((2, CHUNK, 256), F32),
]


def place():
    me = lax.axis_index("rows")
    core = lax.rem(me, 2)
    deep = lax.rem(me // 2, 8)
    plane = me // 16
    return me, core, deep, plane


def device_of(plane, deep, core):
    return (plane * 8 + deep) * 2 + core


def features_of(embed_ref, amp_ref, first):
    part = embed_ref[:, first:first + 128]
    amp = amp_ref[first // 128:first // 128 + 1, :]
    squared = jnp.sum(part * part, axis=0, keepdims=True) * (LOG2E / 64)
    high, low = split_two(part)
    high, low = high.astype(F32), low.astype(F32)
    ones = jnp.ones((1, 128), F32)
    extra = [v.astype(F32) for v in split_three(squared)] + [ones] * 3 + [v.astype(F32) for v in split_three(amp)]
    row = lax.broadcasted_iota(jnp.int32, (64, 128), 0)
    tail = jnp.zeros((64, 128), F32)
    for index, value in enumerate(extra):
        tail = jnp.where(row == index, value, tail)
    one = jnp.concatenate([high, low], axis=0).T.astype(BF16)
    two = jnp.concatenate([high, tail], axis=0).T.astype(BF16)
    return one, two


def gather_kernel(pivots_hbm, embed_hbm, amp_hbm, features_ref, chosen_ref,
                  pivots_ref, embed_ref, amp_ref, loaded, own, column, whole, send1, recv1, send2, recv2, send3, recv3):
    me, core, deep, plane = place()
    loads = [
        pltpu.make_async_copy(pivots_hbm, pivots_ref, loaded.at[0]),
        pltpu.make_async_copy(embed_hbm, embed_ref, loaded.at[1]),
        pltpu.make_async_copy(amp_hbm, amp_ref, loaded.at[2]),
    ]
    for load in loads:
        load.start()
    barrier = pltpu.get_barrier_semaphore()
    peers1 = [device_of(plane, lax.rem(deep + d, 8), core) for d in range(1, 8)]
    peers2 = [device_of(lax.rem(plane + d, 16), deep, core) for d in range(1, 16)]
    other = device_of(plane, deep, 1 - core)
    for peer in peers1 + peers2 + [other]:
        pl.semaphore_signal(barrier, inc=1, device_id=(peer,), device_id_type=MESH)

    for load in loads:
        load.wait()
    lane = lax.broadcasted_iota(jnp.int32, (4, 128), 1)
    pivots = pivots_ref[...]
    owners = pivots >> 12
    offsets = pivots & 4095
    mine = owners == me
    key = lane * 4096 + offsets
    first = jnp.min(jnp.where(mine, key, 128 * 4096 - 1), axis=1, keepdims=True) & 4095
    last = jnp.max(jnp.where(mine, key, 0), axis=1, keepdims=True) & 4095
    lanes = lax.broadcasted_iota(jnp.int32, (64, 128), 1)
    lanes2 = lax.broadcasted_iota(jnp.int32, (128, 128), 1)
    packed = jnp.zeros((128, 128), F32)
    for p in range(4):
        halves = []
        for found in (first, last):
            offset = jnp.broadcast_to(found[p:p + 1, 0:1], (64, 128))
            group = offset >> 7
            part = embed_ref[:, 0:128]
            for b in range(1, 32):
                part = jnp.where(group == b, embed_ref[:, 128 * b:128 * b + 128], part)
            halves.append(jnp.sum(jnp.where(lanes == (offset & 127), part, 0.0), axis=1, keepdims=True))
        packed = jnp.where(lanes2 == p, jnp.concatenate(halves, axis=0), packed)
    tile = packed.T[0:4, :]
    own[...] = tile
    column[deep] = tile

    pl.semaphore_wait(barrier, 23)

    copies1 = []
    for d in range(1, 8):
        copy = pltpu.make_async_remote_copy(
            src_ref=own, dst_ref=column.at[deep], send_sem=send1.at[d - 1], recv_sem=recv1.at[deep],
            device_id=(peers1[d - 1],), device_id_type=MESH)
        copy.start()
        copies1.append(copy)

    wanted = []
    sub2 = lax.broadcasted_iota(jnp.int32, (128, 128), 0)
    for p in range(4):
        row = jnp.broadcast_to(owners[p:p + 1, :], (128, 128)).astype(F32)
        col = row.T
        slot = jnp.sum(jnp.where((row == col) & (lanes2 < sub2), 1.0, 0.0), axis=1, keepdims=True)
        owner = col.astype(jnp.int32)
        spot = (owner & 1) * 128 + (owner >> 1)
        wanted.append((spot, slot))

    for start in range(0, 1024, 128):
        one, two = features_of(embed_ref, amp_ref, start)
        features_ref[start:start + 128, 0:128] = one
        features_ref[start:start + 128, 128:256] = two

    for d in range(1, 8):
        source = lax.rem(deep + d, 8)
        pltpu.make_async_remote_copy(
            src_ref=own, dst_ref=column.at[source], send_sem=send1.at[d - 1], recv_sem=recv1.at[source],
            device_id=(peers1[d - 1],), device_id_type=MESH).wait_recv()
    block = core * 16 + plane
    for p in range(4):
        whole[p, block] = jnp.concatenate([column[z][p:p + 1, :] for z in range(8)], axis=0)

    copies2 = []
    for d in range(1, 16):
        copy = pltpu.make_async_remote_copy(
            src_ref=whole.at[:, block], dst_ref=whole.at[:, block], send_sem=send2.at[d - 1], recv_sem=recv2.at[plane],
            device_id=(peers2[d - 1],), device_id_type=MESH)
        copy.start()
        copies2.append(copy)

    def forward(index, of_plane):
        at = core * 16 + of_plane
        copy = pltpu.make_async_remote_copy(
            src_ref=whole.at[:, at], dst_ref=whole.at[:, at], send_sem=send3.at[index], recv_sem=recv3.at[of_plane],
            device_id=(other,), device_id_type=MESH)
        copy.start()
        return copy

    copies3 = [forward(0, plane)]
    for start in range(1024, 4096, 128):
        one, two = features_of(embed_ref, amp_ref, start)
        features_ref[start:start + 128, 0:128] = one
        features_ref[start:start + 128, 128:256] = two

    for d in range(1, 16):
        source = lax.rem(plane + d, 16)
        at = core * 16 + source
        pltpu.make_async_remote_copy(
            src_ref=whole.at[:, at], dst_ref=whole.at[:, at], send_sem=send2.at[d - 1], recv_sem=recv2.at[source],
            device_id=(peers2[d - 1],), device_id_type=MESH).wait_recv()
        copies3.append(forward(d, source))
    for source in range(16):
        at = (1 - core) * 16 + source
        pltpu.make_async_remote_copy(
            src_ref=whole.at[:, at], dst_ref=whole.at[:, at], send_sem=send3.at[0], recv_sem=recv3.at[source],
            device_id=(other,), device_id_type=MESH).wait_recv()

    for p in range(4):
        spot, slot = wanted[p]
        rows = whole[p].reshape(256, 128)
        parts = jnp.concatenate(split_three(rows), axis=1)
        wide = lax.broadcasted_iota(jnp.int32, (128, 256), 1)
        take = jnp.where(wide == jnp.concatenate([spot, spot], axis=1), 1.0, 0.0).astype(BF16)
        got = jnp.dot(take, parts, preferred_element_type=F32)
        got = got[:, 0:128] + (got[:, 128:256] + got[:, 256:384])
        got = jnp.where(slot > 0.5, pltpu.roll(got, 64, 1), got)
        chosen_ref[128 * p:128 * p + 128, :] = jnp.where(lanes2 < 64, got, 0.0)

    for copy in copies1 + copies2 + copies3:
        copy.wait_send()


def gather(pivots, embed, amp):
    return pl.pallas_call(
        gather_kernel,
        out_shape=(jax.ShapeDtypeStruct((4096, 256), BF16), jax.ShapeDtypeStruct((512, 128), F32)),
        in_specs=[pl.BlockSpec(memory_space=pltpu.HBM)] * 3,
        out_specs=(pl.BlockSpec(memory_space=pltpu.VMEM), pl.BlockSpec(memory_space=pltpu.VMEM)),
        scratch_shapes=[
            pltpu.VMEM((4, 128), jnp.int32), pltpu.VMEM((64, 4096), F32), pltpu.VMEM((32, 128), F32),
            pltpu.SemaphoreType.DMA((3,)),
            pltpu.VMEM((4, 128), F32), pltpu.VMEM((8, 4, 128), F32), pltpu.VMEM((4, 32, 8, 128), F32),
            pltpu.SemaphoreType.DMA((7,)), pltpu.SemaphoreType.DMA((8,)),
            pltpu.SemaphoreType.DMA((15,)), pltpu.SemaphoreType.DMA((16,)),
            pltpu.SemaphoreType.DMA((16,)), pltpu.SemaphoreType.DMA((16,)),
        ],
        compiler_params=pltpu.CompilerParams(collective_id=0, has_side_effects=True, vmem_limit_bytes=32 << 20),
        name="gather_pivots",
    )(pivots, embed, amp)


def product_kernel(features_ref, chosen_ref, amp_ref, factor_ref, residual_ref, sums_ref,
                   matrix, pivots_t, kern, cross, done, wide_amp, squares, inverse_t, upper1, upper2, upper3,
                   raw_first, raw_near, raw_far, staged, sems):
    prepare(chosen_ref[...], matrix, pivots_t)
    copies = []

    def sent(p, j):
        if j % 4 == 3:
            rows = pl.ds(CHUNK * (j - 3), 4 * CHUNK)
            copy = pltpu.make_async_copy(
                staged.at[p, rows], factor_ref.at[rows, pl.ds(128 * p, 128)], sems.at[4 * p + j // 4])
            copy.start()
            copies.append(copy)

    sums = factorise(features_ref, amp_ref, matrix, pivots_t, kern, cross, done, wide_amp, squares, inverse_t,
                     (None, upper1, upper2, upper3), raw_first, raw_near, raw_far, staged, residual_ref, sent)
    for p in range(4):
        sums_ref[8 * p:8 * p + 8, :] = sums[p]
    for copy in copies:
        copy.wait()


def product(features, chosen, amp):
    return pl.pallas_call(
        product_kernel,
        out_shape=(jax.ShapeDtypeStruct((4096, 512), F32), jax.ShapeDtypeStruct((32, 128), F32),
                   jax.ShapeDtypeStruct((32, 128), F32)),
        in_specs=[pl.BlockSpec(memory_space=pltpu.VMEM)] * 3,
        out_specs=(pl.BlockSpec(memory_space=pltpu.HBM), pl.BlockSpec(memory_space=pltpu.VMEM),
                   pl.BlockSpec(memory_space=pltpu.VMEM)),
        scratch_shapes=SCRATCH + [pltpu.VMEM((4, 4096, 128), F32), pltpu.SemaphoreType.DMA((16,))],
        compiler_params=pltpu.CompilerParams(vmem_limit_bytes=50 << 20),
        name="cholesky_product",
    )(features, chosen, amp)


def sums_kernel(points, sums_ref, amp_ref, means_ref, own, land1, middle, land2, send1, recv1, send2, recv2):
    me, core, deep, plane = place()
    line = deep * 2 + core
    barrier = pltpu.get_barrier_semaphore()
    peers1 = [plane * 16 + lax.rem(line + d, 16) for d in range(1, 16)]
    peers2 = [lax.rem(plane + d, 16) * 16 + line for d in range(1, 16)]
    for peer in peers1 + peers2:
        pl.semaphore_signal(barrier, inc=1, device_id=(peer,), device_id_type=MESH)

    lane = lax.broadcasted_iota(jnp.int32, (8, 128), 1)
    total = jnp.sum(amp_ref[...] * amp_ref[...])
    value = jnp.zeros((8, 128), F32)
    for p in range(4):
        total = total - jnp.sum(sums_ref[8 * p:8 * p + 8, :])
        value = jnp.where(lane == p, total, value)
    own[...] = value
    land1[line] = value
    pl.semaphore_wait(barrier, 30)

    def exchange(source, land, at, peers, send, recv):
        copies = []
        for d in range(1, 16):
            copy = pltpu.make_async_remote_copy(
                src_ref=source, dst_ref=land.at[at], send_sem=send.at[d - 1], recv_sem=recv.at[at],
                device_id=(peers[d - 1],), device_id_type=MESH)
            copy.start()
            copies.append(copy)
        for d in range(1, 16):
            origin = lax.rem(at + d, 16)
            pltpu.make_async_remote_copy(
                src_ref=source, dst_ref=land.at[origin], send_sem=send.at[d - 1], recv_sem=recv.at[origin],
                device_id=(peers[d - 1],), device_id_type=MESH).wait_recv()
        return copies, jnp.sum(land[...], axis=0)

    copies1, value = exchange(own, land1, line, peers1, send1, recv1)
    middle[...] = value
    land2[plane] = value
    copies2, value = exchange(middle, land2, plane, peers2, send2, recv2)
    means_ref[...] = value[0:1, 0:4] * (1.0 / points)
    for copy in copies1 + copies2:
        copy.wait_send()


def mean_sums(sums, amp, points):
    return pl.pallas_call(
        functools.partial(sums_kernel, points),
        out_shape=jax.ShapeDtypeStruct((1, 4), F32),
        in_specs=[pl.BlockSpec(memory_space=pltpu.VMEM)] * 2,
        out_specs=pl.BlockSpec(memory_space=pltpu.VMEM),
        scratch_shapes=[
            pltpu.VMEM((8, 128), F32), pltpu.VMEM((16, 8, 128), F32), pltpu.VMEM((8, 128), F32),
            pltpu.VMEM((16, 8, 128), F32),
            pltpu.SemaphoreType.DMA((15,)), pltpu.SemaphoreType.DMA((16,)),
            pltpu.SemaphoreType.DMA((15,)), pltpu.SemaphoreType.DMA((16,)),
        ],
        compiler_params=pltpu.CompilerParams(collective_id=1, has_side_effects=True),
        name="sum_residuals",
    )(sums, amp)


def local(embed, amplitude, pivots):
    amp = amplitude.reshape(32, 128)
    features, chosen = gather(pivots, embed.T, amp)
    factor, residual, sums = product(features, chosen, amp)
    means = mean_sums(sums, amp, 4096 * lax.axis_size("rows"))
    return factor, residual.reshape(4096), means.reshape(4)


def solution(mesh):
    return jax.shard_map(
        local,
        mesh=mesh,
        in_specs=(P("rows", None), P("rows"), P()),
        out_specs=(P("rows", None), P("rows"), P()),
        check_vma=False,
    )
```

```python
import functools

import jax
import jax.numpy as jnp
from jax import lax
from jax.experimental import pallas as pl
from jax.experimental.pallas import tpu as pltpu
from jax.sharding import PartitionSpec as P

HI = lax.Precision.HIGHEST
F32 = jnp.float32

LOG2E = 1.4426950408889634
MESH = pl.DeviceIdType.MESH
BF16 = jnp.bfloat16


def spread_row(block, row):
    return jnp.broadcast_to(block[row:row + 1, :], (8, 128))


def spread_col(block, col):
    return jnp.broadcast_to(block[:, col:col + 1], (8, 128))


def tree(terms):
    while len(terms) > 1:
        terms = [a + b for a, b in zip(terms[::2], terms[1::2])] + ([terms[-1]] if len(terms) % 2 else [])
    return terms[0]


def eliminate_rows(blocks, base, work, step):
    lane = lax.broadcasted_iota(jnp.int32, (8, 128), 1)
    sub = lax.broadcasted_iota(jnp.int32, (8, 128), 0)
    count = len(blocks)
    blocks = list(blocks)
    diag = [spread_col(blocks[0], base + k) for k in range(8)]
    for j in range(count):
        at = base + 8 * j
        inside = (lane >= at) & (lane < at + 8)
        below = {b: [spread_col(blocks[b], at + k) for k in range(8)] for b in range(j + 1, count)}
        following = [spread_col(blocks[j + 1], at + 8 + k) for k in range(8)] if j + 1 < count else None
        rest = jnp.where(inside, jnp.where(lane - at == sub, 1.0, 0.0), blocks[j])
        rows = []
        for k in range(8):
            scale = lax.rsqrt(spread_row(diag[k], k))
            low = diag[k] * scale
            row = spread_row(rest, k) * scale
            rows.append(row)
            if k < 7:
                rest = rest - low * row
            for b in below:
                below[b][k] = below[b][k] * scale
            for m in range(k + 1, 8):
                factor = spread_row(low, m)
                diag[m] = diag[m] - low * factor
                for b in below:
                    below[b][m] = below[b][m] - below[b][k] * factor
            step()
        out = rows[0]
        for k in range(1, 8):
            out = jnp.where(sub == k, rows[k], out)
        blocks[j] = out
        if j + 1 < count:
            first = below[j + 1]
            diag = [following[k] - tree([first[m] * spread_row(first[m], k) for m in range(8)]) for k in range(8)]
        for b in below:
            blocks[b] = jnp.where(inside, 0.0, blocks[b]) - tree([below[b][k] * rows[k] for k in range(8)])
        work(at // 8)
    return blocks


def eliminate(blocks, work, step, width=64):
    lane = lax.broadcasted_iota(jnp.int32, (8, 128), 1)
    blocks = list(blocks)
    group = width // 8
    for base in range(0, 128, width):
        first = base // 8
        blocks[first:first + group] = eliminate_rows(blocks[first:first + group], base, work, step)
        if base + width < 128:
            rows = jnp.concatenate(blocks[first:first + group], axis=0)
            row = lax.broadcasted_iota(jnp.int32, (width, 128), 0) + base
            col = lax.broadcasted_iota(jnp.int32, (width, 128), 1)
            lower = jnp.where((col > row) & (col < base + width), 0.0, rows)
            change = lax.dot_general(rows, lower, (((0,), (0,)), ((), ())), precision=HI, preferred_element_type=F32)
            inside = (lane >= base) & (lane < base + width)
            for b in range(first + group, 16):
                blocks[b] = jnp.where(inside, 0.0, blocks[b]) - change[8 * b:8 * b + 8, :]
    return blocks


def split_two(value):
    high = value.astype(BF16)
    return high, (value - high.astype(F32)).astype(BF16)


def split_three(value):
    high = value.astype(BF16)
    left = value - high.astype(F32)
    middle = left.astype(BF16)
    return high, middle, (left - middle.astype(F32)).astype(BF16)


def both_parts(value):
    both = jnp.concatenate(split_two(value), axis=1)
    return jnp.concatenate([both, both], axis=0)


def halves(value):
    return value[:, 0:128] + value[:, 128:256]


def prepare(chosen, matrix, pivots_t):
    lane = lax.broadcasted_iota(jnp.int32, (512, 128), 1)
    squared = jnp.sum(chosen * chosen, axis=1, keepdims=True) * (LOG2E / 64)
    scaled = chosen * (2 * LOG2E / 64)
    left = jnp.where(lane < 64, chosen, jnp.where(lane == 64, squared, jnp.where(lane == 65, 1.0, 0.0)))
    right = jnp.where(lane < 64, scaled, jnp.where(lane == 64, -1.0, jnp.where(lane == 65, -squared, 0.0)))
    power = lax.dot_general(left, right, (((1,), (1,)), ((), ())), precision=HI, preferred_element_type=F32)
    matrix[...] = jnp.exp2(jnp.minimum(power, 0.0))
    high, low = [v.astype(F32) for v in split_two(scaled)]
    extra = [jnp.full((512, 1), -1.0, F32)] * 3 + [-v.astype(F32) for v in split_three(squared)]
    extra += [jnp.full((512, 1), 1.0, F32)] * 3
    one = jnp.where(lane < 64, high, pltpu.roll(high, 64, 1))
    two = jnp.where(lane < 64, low, 0.0)
    for index, value in enumerate(extra):
        two = jnp.where(lane == 64 + index, value, two)
    pivots_t[0:128, 0:512] = one.T.astype(BF16)
    pivots_t[128:256, 0:512] = two.T.astype(BF16)
    row = lax.broadcasted_iota(jnp.int32, (256, 128), 0)
    pivots_t[:, 512:640] = jnp.where((row >= 198) & (row < 201), 1.0, 0.0).astype(BF16)


CHUNK = 256
CHUNKS = 4096 // CHUNK
PIECE = 32
PER_STEP = 2


def factorise(features_ref, amp_ref, matrix, pivots_t, kern, cross, done, squares, inverse_t, upper,
              raw_first, raw_near, raw_far, factor_ref, residual_ref):
    sums = [[] for _ in range(4)]
    pending = []

    def step(count=PER_STEP):
        for _ in range(min(count, len(pending))):
            pending.pop(0)()

    def pieces(j):
        return [(slice(CHUNK * j + r, CHUNK * j + r + PIECE), slice(r, r + PIECE)) for r in range(0, CHUNK, PIECE)]

    def start_first(j):
        raw_first[j % 2] = jnp.dot(
            features_ref[CHUNK * j:CHUNK * j + CHUNK, :], pivots_t[...], preferred_element_type=F32)

    def end_first(j, at, part):
        top = raw_first[j % 2, part, 512:640]
        near = [jnp.exp2(jnp.minimum(raw_first[j % 2, part, 128 * q:128 * q + 128], top)) for q in range(4)]
        cross[at, :] = jnp.concatenate(split_two(near[0]), axis=1)
        kern[at, :] = jnp.concatenate(near[1:], axis=1)

    def start_near(p, j):
        raw_near[j % 2] = jnp.dot(
            cross[CHUNK * j:CHUNK * j + CHUNK, :], inverse_t[p], preferred_element_type=F32)

    def end_near(p, j, at, part):
        got = halves(raw_near[j % 2, part, :])
        factor_ref[at, 128 * p:128 * p + 128] = got
        square = got * got
        sums[p].append(tree([square[8 * b:8 * b + 8, :] for b in range(PIECE // 8)]))
        if p < 3:
            squares[at, :] = square if p == 0 else squares[at, :] + square
            done[at, 256 * p:256 * p + 256] = jnp.concatenate(split_two(got), axis=1)
        else:
            squares[at, :] = squares[at, :] + square

    def start_far(p, j):
        raw_far[j % 2] = jnp.dot(
            done[CHUNK * j:CHUNK * j + CHUNK, 0:256 * (p + 1)], upper[p + 1][...], preferred_element_type=F32)

    def end_far(p, j, at, part):
        rest = kern[at, 128 * p:128 * p + 128] - halves(raw_far[j % 2, part, :])
        cross[at, :] = jnp.concatenate(split_two(rest), axis=1)

    def residual_of(j):
        both = jnp.concatenate(split_two(squares[CHUNK * j:CHUNK * j + CHUNK, :]), axis=1)
        spent = lax.dot_general(jnp.ones((8, 256), BF16), both, (((1,), (1,)), ((), ())), preferred_element_type=F32)
        for b in range(CHUNK // 128):
            row = j * (CHUNK // 128) + b
            own = amp_ref[row:row + 1, :]
            residual_ref[row:row + 1, :] = own * own - spent[0:1, 128 * b:128 * b + 128]

    def schedule(t):
        if 0 <= t < 16:
            start_first(t)
        if 1 <= t < 17:
            pending.extend(functools.partial(end_first, t - 1, *piece) for piece in pieces(t - 1))
        if 16 <= t < 80:
            start_near(t // 16 - 1, t % 16)
        if 18 <= t < 66:
            p, j = (t - 2) // 16 - 1, (t - 2) % 16
            pending.extend(functools.partial(end_far, p, j, *piece) for piece in pieces(j))
        if 17 <= t < 81:
            p, j = (t - 1) // 16 - 1, (t - 1) % 16
            pending.extend(functools.partial(end_near, p, j, *piece) for piece in pieces(j))
            if p < 3:
                pending.append(functools.partial(start_far, p, j))
        if 66 <= t < 82:
            pending.append(functools.partial(residual_of, t - 66))

    lane = lax.broadcasted_iota(jnp.int32, (128, 128), 1)
    sub = lax.broadcasted_iota(jnp.int32, (128, 128), 0)
    for p in range(4):
        lo = 128 * p

        def work(j):
            step(len(pending))
            if j < 15:
                schedule(16 * p + j + 1)

        schedule(16 * p)
        got = eliminate([matrix[lo + 8 * b:lo + 8 * b + 8, lo:lo + 128] for b in range(16)], work, step)
        inverse = jnp.where(lane <= sub, jnp.concatenate(got, axis=0), 0.0)
        inverse_t[p] = both_parts(inverse.T)
        if p < 3:
            right = jnp.dot(inverse, matrix[lo:lo + 128, lo + 128:], precision=HI, preferred_element_type=F32)
            for q in range(p + 1, 4):
                part = right[:, 128 * (q - p - 1):128 * (q - p)]
                matrix[128 * q:128 * q + 128, 128 * q:] -= lax.dot_general(
                    part, right[:, 128 * (q - p - 1):], (((0,), (0,)), ((), ())), precision=HI,
                    preferred_element_type=F32)
                upper[q][256 * p:256 * p + 256, :] = both_parts(part)
    for t in range(64, 82):
        schedule(t)
        step(len(pending))
    return [tree(parts) for parts in sums]


SCRATCH = [
    pltpu.VMEM((512, 512), F32), pltpu.VMEM((256, 640), BF16), pltpu.VMEM((4096, 384), F32),
    pltpu.VMEM((4096, 256), BF16), pltpu.VMEM((4096, 768), BF16), pltpu.VMEM((4096, 128), F32),
    pltpu.VMEM((4, 256, 256), BF16),
    pltpu.VMEM((256, 256), BF16), pltpu.VMEM((512, 256), BF16), pltpu.VMEM((768, 256), BF16),
    pltpu.VMEM((2, CHUNK, 640), F32), pltpu.VMEM((2, CHUNK, 256), F32), pltpu.VMEM((2, CHUNK, 256), F32),
]


def place():
    me = lax.axis_index("rows")
    core = lax.rem(me, 2)
    deep = lax.rem(me // 2, 8)
    plane = me // 16
    return me, core, deep, plane


def device_of(plane, deep, core):
    return (plane * 8 + deep) * 2 + core


def features_of(embed_ref, amp_ref, first):
    part = embed_ref[:, first:first + 128]
    amp = jnp.log2(amp_ref[first // 128:first // 128 + 1, :])
    squared = jnp.sum(part * part, axis=0, keepdims=True) * (LOG2E / 64)
    high, low = split_two(part)
    high, low = high.astype(F32), low.astype(F32)
    ones = jnp.ones((1, 128), F32)
    extra = [v.astype(F32) for v in split_three(squared)] + [ones] * 3 + [v.astype(F32) for v in split_three(amp)]
    row = lax.broadcasted_iota(jnp.int32, (64, 128), 0)
    tail = jnp.zeros((64, 128), F32)
    for index, value in enumerate(extra):
        tail = jnp.where(row == index, value, tail)
    one = jnp.concatenate([high, low], axis=0).T.astype(BF16)
    two = jnp.concatenate([high, tail], axis=0).T.astype(BF16)
    return one, two


def whole_kernel(points, pivots_hbm, embed_hbm, amp_hbm, factor_ref, residual_ref, means_ref,
                 pivots_ref, embed_ref, amp_ref, loaded, features_ref, chosen_ref,
                 own, column, whole, send1, recv1, send2, recv2, send3, recv3,
                 mine1, mine2, land2, mine3, land3, total_sems,
                 matrix, pivots_t, kern, cross, done, squares, inverse_t, upper1, upper2, upper3,
                 raw_first, raw_near, raw_far):
    me, core, deep, plane = place()
    loads = [
        pltpu.make_async_copy(pivots_hbm, pivots_ref, loaded.at[0]),
        pltpu.make_async_copy(embed_hbm, embed_ref, loaded.at[1]),
        pltpu.make_async_copy(amp_hbm, amp_ref, loaded.at[2]),
    ]
    for load in loads:
        load.start()
    barrier = pltpu.get_barrier_semaphore()
    peers1 = [device_of(plane, lax.rem(deep + d, 8), core) for d in range(1, 8)]
    peers2 = [device_of(lax.rem(plane + d, 16), deep, core) for d in range(1, 16)]
    other = device_of(plane, deep, 1 - core)
    for peer in peers1 + peers2 + [other]:
        pl.semaphore_signal(barrier, inc=1, device_id=(peer,), device_id_type=MESH)

    for load in loads:
        load.wait()
    lane = lax.broadcasted_iota(jnp.int32, (4, 128), 1)
    pivots = pivots_ref[...]
    owners = pivots >> 12
    offsets = pivots & 4095
    mine = owners == me
    key = lane * 4096 + offsets
    first = jnp.min(jnp.where(mine, key, 128 * 4096 - 1), axis=1, keepdims=True) & 4095
    last = jnp.max(jnp.where(mine, key, 0), axis=1, keepdims=True) & 4095
    lanes = lax.broadcasted_iota(jnp.int32, (64, 128), 1)
    lanes2 = lax.broadcasted_iota(jnp.int32, (128, 128), 1)
    packed = jnp.zeros((128, 128), F32)
    for p in range(4):
        halves = []
        for found in (first, last):
            offset = jnp.broadcast_to(found[p:p + 1, 0:1], (64, 128))
            group = offset >> 7
            part = embed_ref[:, 0:128]
            for b in range(1, 32):
                part = jnp.where(group == b, embed_ref[:, 128 * b:128 * b + 128], part)
            halves.append(jnp.sum(jnp.where(lanes == (offset & 127), part, 0.0), axis=1, keepdims=True))
        packed = jnp.where(lanes2 == p, jnp.concatenate(halves, axis=0), packed)
    tile = packed.T[0:4, :]
    own[...] = tile
    column[deep] = tile

    pl.semaphore_wait(barrier, 23)

    copies1 = []
    for d in range(1, 8):
        copy = pltpu.make_async_remote_copy(
            src_ref=own, dst_ref=column.at[deep], send_sem=send1.at[d - 1], recv_sem=recv1.at[deep],
            device_id=(peers1[d - 1],), device_id_type=MESH)
        copy.start()
        copies1.append(copy)

    wanted = []
    sub2 = lax.broadcasted_iota(jnp.int32, (128, 128), 0)
    for p in range(4):
        row = jnp.broadcast_to(owners[p:p + 1, :], (128, 128)).astype(F32)
        col = row.T
        slot = jnp.sum(jnp.where((row == col) & (lanes2 < sub2), 1.0, 0.0), axis=1, keepdims=True)
        owner = col.astype(jnp.int32)
        spot = (owner & 1) * 128 + (owner >> 1)
        wanted.append((spot, slot))

    for start in range(0, 1024, 128):
        one, two = features_of(embed_ref, amp_ref, start)
        features_ref[start:start + 128, 0:128] = one
        features_ref[start:start + 128, 128:256] = two

    for d in range(1, 8):
        source = lax.rem(deep + d, 8)
        pltpu.make_async_remote_copy(
            src_ref=own, dst_ref=column.at[source], send_sem=send1.at[d - 1], recv_sem=recv1.at[source],
            device_id=(peers1[d - 1],), device_id_type=MESH).wait_recv()
    block = core * 16 + plane
    for p in range(4):
        whole[p, block] = jnp.concatenate([column[z][p:p + 1, :] for z in range(8)], axis=0)

    copies2 = []
    for d in range(1, 16):
        copy = pltpu.make_async_remote_copy(
            src_ref=whole.at[:, block], dst_ref=whole.at[:, block], send_sem=send2.at[d - 1], recv_sem=recv2.at[plane],
            device_id=(peers2[d - 1],), device_id_type=MESH)
        copy.start()
        copies2.append(copy)

    def forward(index, of_plane):
        at = core * 16 + of_plane
        copy = pltpu.make_async_remote_copy(
            src_ref=whole.at[:, at], dst_ref=whole.at[:, at], send_sem=send3.at[index], recv_sem=recv3.at[of_plane],
            device_id=(other,), device_id_type=MESH)
        copy.start()
        return copy

    copies3 = [forward(0, plane)]
    for start in range(1024, 4096, 128):
        one, two = features_of(embed_ref, amp_ref, start)
        features_ref[start:start + 128, 0:128] = one
        features_ref[start:start + 128, 128:256] = two

    for d in range(1, 16):
        source = lax.rem(plane + d, 16)
        at = core * 16 + source
        pltpu.make_async_remote_copy(
            src_ref=whole.at[:, at], dst_ref=whole.at[:, at], send_sem=send2.at[d - 1], recv_sem=recv2.at[source],
            device_id=(peers2[d - 1],), device_id_type=MESH).wait_recv()
        copies3.append(forward(d, source))
    for source in range(16):
        at = (1 - core) * 16 + source
        pltpu.make_async_remote_copy(
            src_ref=whole.at[:, at], dst_ref=whole.at[:, at], send_sem=send3.at[0], recv_sem=recv3.at[source],
            device_id=(other,), device_id_type=MESH).wait_recv()

    for p in range(4):
        spot, slot = wanted[p]
        rows = whole[p].reshape(256, 128)
        parts = jnp.concatenate(split_three(rows), axis=1)
        wide = lax.broadcasted_iota(jnp.int32, (128, 256), 1)
        take = jnp.where(wide == jnp.concatenate([spot, spot], axis=1), 1.0, 0.0).astype(BF16)
        got = jnp.dot(take, parts, preferred_element_type=F32)
        got = got[:, 0:128] + (got[:, 128:256] + got[:, 256:384])
        got = jnp.where(slot > 0.5, pltpu.roll(got, 64, 1), got)
        chosen_ref[128 * p:128 * p + 128, :] = jnp.where(lanes2 < 64, got, 0.0)

    for copy in copies1 + copies2 + copies3:
        copy.wait_send()

    prepare(chosen_ref[...], matrix, pivots_t)
    sums = factorise(features_ref, amp_ref, matrix, pivots_t, kern, cross, done, squares, inverse_t,
                     (None, upper1, upper2, upper3), raw_first, raw_near, raw_far, factor_ref, residual_ref)

    lane8 = lax.broadcasted_iota(jnp.int32, (8, 128), 1)
    total = jnp.sum(amp_ref[...] * amp_ref[...])
    value = jnp.zeros((8, 128), F32)
    for p in range(4):
        total = total - jnp.sum(sums[p])
        value = jnp.where(lane8 == p, total, value)

    mine1[core] = value
    copy = pltpu.make_async_remote_copy(
        src_ref=mine1.at[core], dst_ref=mine1.at[core], send_sem=total_sems.at[0], recv_sem=total_sems.at[1],
        device_id=(other,), device_id_type=MESH)
    copy.start()
    copy.wait_recv()
    value = mine1[0] + mine1[1]
    copies4 = [copy]

    def exchange(value, source, land, at, size, peers, first):
        source[...] = value
        land[at] = value
        copies = []
        for d in range(1, size):
            copy = pltpu.make_async_remote_copy(
                src_ref=source, dst_ref=land.at[at], send_sem=total_sems.at[first + d],
                recv_sem=total_sems.at[first + size + at], device_id=(peers[d - 1],), device_id_type=MESH)
            copy.start()
            copies.append(copy)
        for d in range(1, size):
            origin = lax.rem(at + d, size)
            pltpu.make_async_remote_copy(
                src_ref=source, dst_ref=land.at[origin], send_sem=total_sems.at[first + d],
                recv_sem=total_sems.at[first + size + origin], device_id=(peers[d - 1],),
                device_id_type=MESH).wait_recv()
        return copies, jnp.sum(land[...], axis=0)

    copies5, value = exchange(value, mine2, land2, deep, 8, peers1, 2)
    copies6, value = exchange(value, mine3, land3, plane, 16, peers2, 18)
    means_ref[...] = value[0:1, 0:4] * (1.0 / points)
    for copy in copies4 + copies5 + copies6:
        copy.wait_send()


def write_kernel(factor_ref, residual_ref, means_ref, factor_hbm, residual_hbm, means_hbm, sems):
    copies = [
        pltpu.make_async_copy(residual_ref, residual_hbm, sems.at[8]),
        pltpu.make_async_copy(means_ref, means_hbm, sems.at[9]),
    ]
    for part in range(8):
        rows = pl.ds(512 * part, 512)
        copies.append(pltpu.make_async_copy(factor_ref.at[rows], factor_hbm.at[rows], sems.at[part]))
    for copy in copies:
        copy.start()
    for copy in copies:
        copy.wait()


def local(embed, amplitude, pivots):
    points = 4096 * lax.axis_size("rows")
    factor, residual, means = pl.pallas_call(
        functools.partial(whole_kernel, points),
        out_shape=(jax.ShapeDtypeStruct((4096, 512), F32), jax.ShapeDtypeStruct((32, 128), F32),
                   jax.ShapeDtypeStruct((1, 4), F32)),
        in_specs=[pl.BlockSpec(memory_space=pltpu.HBM)] * 3,
        out_specs=[pl.BlockSpec(memory_space=pltpu.VMEM)] * 3,
        scratch_shapes=[
            pltpu.VMEM((4, 128), jnp.int32), pltpu.VMEM((64, 4096), F32), pltpu.VMEM((32, 128), F32),
            pltpu.SemaphoreType.DMA((3,)),
            pltpu.VMEM((4096, 256), BF16), pltpu.VMEM((512, 128), F32),
            pltpu.VMEM((4, 128), F32), pltpu.VMEM((8, 4, 128), F32), pltpu.VMEM((4, 32, 8, 128), F32),
            pltpu.SemaphoreType.DMA((7,)), pltpu.SemaphoreType.DMA((8,)),
            pltpu.SemaphoreType.DMA((15,)), pltpu.SemaphoreType.DMA((16,)),
            pltpu.SemaphoreType.DMA((16,)), pltpu.SemaphoreType.DMA((16,)),
            pltpu.VMEM((2, 8, 128), F32), pltpu.VMEM((8, 128), F32),
            pltpu.VMEM((8, 8, 128), F32), pltpu.VMEM((8, 128), F32), pltpu.VMEM((16, 8, 128), F32),
            pltpu.SemaphoreType.DMA((50,)),
        ] + SCRATCH,
        compiler_params=pltpu.CompilerParams(collective_id=0, has_side_effects=True, vmem_limit_bytes=45000000),
        name="pivoted_cholesky",
    )(pivots, embed.T, amplitude.reshape(32, 128))
    factor, residual, means = pl.pallas_call(
        write_kernel,
        out_shape=(jax.ShapeDtypeStruct((4096, 512), F32), jax.ShapeDtypeStruct((32, 128), F32),
                   jax.ShapeDtypeStruct((1, 4), F32)),
        in_specs=[pl.BlockSpec(memory_space=pltpu.VMEM)] * 3,
        out_specs=[pl.BlockSpec(memory_space=pltpu.HBM)] * 3,
        scratch_shapes=[pltpu.SemaphoreType.DMA((10,))],
        compiler_params=pltpu.CompilerParams(vmem_limit_bytes=1 << 20),
        name="write_out",
    )(factor, residual, means)
    return factor, residual.reshape(4096), means.reshape(4)


def solution(mesh):
    return jax.shard_map(
        local,
        mesh=mesh,
        in_specs=(P("rows", None), P("rows"), P()),
        out_specs=(P("rows", None), P("rows"), P()),
        check_vma=False,
    )
```

```python
import functools

import jax
import jax.numpy as jnp
from jax import lax
from jax.experimental import pallas as pl
from jax.experimental.pallas import tpu as pltpu
from jax.sharding import PartitionSpec as P

HI = lax.Precision.HIGHEST
F32 = jnp.float32

LOG2E = 1.4426950408889634
MESH = pl.DeviceIdType.MESH
BF16 = jnp.bfloat16


def spread_row(block, row):
    return jnp.broadcast_to(block[row:row + 1, :], (8, 128))


def spread_col(block, col):
    return jnp.broadcast_to(block[:, col:col + 1], (8, 128))


def tree(terms):
    while len(terms) > 1:
        terms = [a + b for a, b in zip(terms[::2], terms[1::2])] + ([terms[-1]] if len(terms) % 2 else [])
    return terms[0]


def eliminate_rows(blocks, base, work, step):
    lane = lax.broadcasted_iota(jnp.int32, (8, 128), 1)
    sub = lax.broadcasted_iota(jnp.int32, (8, 128), 0)
    count = len(blocks)
    blocks = list(blocks)
    diag = [spread_col(blocks[0], base + k) for k in range(8)]
    for j in range(count):
        at = base + 8 * j
        inside = (lane >= at) & (lane < at + 8)
        below = {b: [spread_col(blocks[b], at + k) for k in range(8)] for b in range(j + 1, count)}
        following = [spread_col(blocks[j + 1], at + 8 + k) for k in range(8)] if j + 1 < count else None
        rest = jnp.where(inside, jnp.where(lane - at == sub, 1.0, 0.0), blocks[j])
        rows = []
        for k in range(8):
            scale = lax.rsqrt(spread_row(diag[k], k))
            low = diag[k] * scale
            row = spread_row(rest, k) * scale
            rows.append(row)
            if k < 7:
                rest = rest - low * row
            for b in below:
                below[b][k] = below[b][k] * scale
            for m in range(k + 1, 8):
                factor = spread_row(low, m)
                diag[m] = diag[m] - low * factor
                for b in below:
                    below[b][m] = below[b][m] - below[b][k] * factor
            step()
        out = rows[0]
        for k in range(1, 8):
            out = jnp.where(sub == k, rows[k], out)
        blocks[j] = out
        if j + 1 < count:
            first = below[j + 1]
            diag = [following[k] - tree([first[m] * spread_row(first[m], k) for m in range(8)]) for k in range(8)]
        for b in below:
            blocks[b] = jnp.where(inside, 0.0, blocks[b]) - tree([below[b][k] * rows[k] for k in range(8)])
        work(at // 8)
    return blocks


def eliminate(blocks, work, step, width=64):
    lane = lax.broadcasted_iota(jnp.int32, (8, 128), 1)
    blocks = list(blocks)
    group = width // 8
    for base in range(0, 128, width):
        first = base // 8
        blocks[first:first + group] = eliminate_rows(blocks[first:first + group], base, work, step)
        if base + width < 128:
            rows = jnp.concatenate(blocks[first:first + group], axis=0)
            row = lax.broadcasted_iota(jnp.int32, (width, 128), 0) + base
            col = lax.broadcasted_iota(jnp.int32, (width, 128), 1)
            lower = jnp.where((col > row) & (col < base + width), 0.0, rows)
            change = lax.dot_general(rows, lower, (((0,), (0,)), ((), ())), precision=HI, preferred_element_type=F32)
            inside = (lane >= base) & (lane < base + width)
            for b in range(first + group, 16):
                blocks[b] = jnp.where(inside, 0.0, blocks[b]) - change[8 * b:8 * b + 8, :]
    return blocks


def split_two(value):
    high = value.astype(BF16)
    return high, (value - high.astype(F32)).astype(BF16)


def split_three(value):
    high = value.astype(BF16)
    left = value - high.astype(F32)
    middle = left.astype(BF16)
    return high, middle, (left - middle.astype(F32)).astype(BF16)


def both_parts(value):
    both = jnp.concatenate(split_two(value), axis=1)
    return jnp.concatenate([both, both], axis=0)


def halves(value):
    return value[:, 0:128] + value[:, 128:256]


def prepare(chosen_ref, matrix, pivots_t):
    lane = lax.broadcasted_iota(jnp.int32, (128, 128), 1)
    lefts, rights = [], []

    def beside(first, second):
        return jnp.where(lane < 64, first, pltpu.roll(second, 64, 1))

    def with_tail(first, values):
        out = jnp.where(lane < 64, first, 0.0)
        for index, value in enumerate(values):
            out = jnp.where(lane == 64 + index, value, out)
        return out

    def block(p, q, size):
        right = jnp.concatenate(rights[q:q + size], axis=0)
        power = lax.dot_general(lefts[p], right, (((1,), (1,)), ((), ())), preferred_element_type=F32)
        matrix[128 * p:128 * p + 128, 128 * q:128 * (q + size)] = jnp.exp2(jnp.minimum(power, 0.0))

    for p in range(4):
        at = slice(128 * p, 128 * p + 128)
        chosen = chosen_ref[at, :]
        squared = jnp.sum(chosen * chosen, axis=1, keepdims=True) * (LOG2E / 64)
        squares = [part.astype(F32) for part in split_three(squared)]
        high, middle, low = [part.astype(F32) for part in split_three(chosen)]
        left = [beside(high, middle), with_tail(high, squares + [1.0] * 3), beside(middle, high), with_tail(low, [])]
        lefts.append(jnp.concatenate([part.astype(BF16) for part in left], axis=1))
        high, middle, low = [part.astype(F32) for part in split_three(chosen * (2 * LOG2E / 64))]
        one = beside(high, high)
        two = with_tail(middle, [-1.0] * 3 + [-part for part in squares] + [1.0] * 3)
        right = [one, two, beside(middle, low), with_tail(high, [])]
        rights.append(jnp.concatenate([part.astype(BF16) for part in right], axis=1))
        if p == 0:
            block(0, 0, 1)
        pivots_t[0:128, at] = one.T.astype(BF16)
        pivots_t[128:256, at] = two.T.astype(BF16)
    row = lax.broadcasted_iota(jnp.int32, (256, 128), 0)
    pivots_t[:, 512:640] = jnp.where((row >= 198) & (row < 201), 1.0, 0.0).astype(BF16)
    return [functools.partial(block, *which) for which in ((0, 1, 3), (1, 1, 3), (2, 2, 2), (3, 3, 1))]


CHUNK = 256
CHUNKS = 4096 // CHUNK
PIECE = 32
PER_STEP = 2


def factorise(features_ref, amp_ref, matrix, pivots_t, kern, cross, done, squares, inverse_t, upper,
              raw_first, raw_near, raw_far, factor_ref, residual_ref, later):
    sums = [[] for _ in range(4)]
    pending = []

    def step(count=PER_STEP):
        for _ in range(min(count, len(pending))):
            pending.pop(0)()

    def pieces(j):
        return [(slice(CHUNK * j + r, CHUNK * j + r + PIECE), slice(r, r + PIECE)) for r in range(0, CHUNK, PIECE)]

    def start_first(j):
        raw_first[j % 2] = jnp.dot(
            features_ref[CHUNK * j:CHUNK * j + CHUNK, :], pivots_t[...], preferred_element_type=F32)

    def end_first(j, at, part):
        top = raw_first[j % 2, part, 512:640]
        near = [jnp.exp2(jnp.minimum(raw_first[j % 2, part, 128 * q:128 * q + 128], top)) for q in range(4)]
        cross[at, :] = jnp.concatenate(split_two(near[0]), axis=1)
        kern[at, :] = jnp.concatenate(near[1:], axis=1)

    def start_near(p, j):
        raw_near[j % 2] = jnp.dot(
            cross[CHUNK * j:CHUNK * j + CHUNK, :], inverse_t[p], preferred_element_type=F32)

    def end_near(p, j, at, part):
        got = halves(raw_near[j % 2, part, :])
        factor_ref[at, 128 * p:128 * p + 128] = got
        square = got * got
        sums[p].append(tree([square[8 * b:8 * b + 8, :] for b in range(PIECE // 8)]))
        if p < 3:
            squares[at, :] = square if p == 0 else squares[at, :] + square
            done[at, 256 * p:256 * p + 256] = jnp.concatenate(split_two(got), axis=1)
        else:
            squares[at, :] = squares[at, :] + square

    def start_far(p, j):
        raw_far[j % 2] = jnp.dot(
            done[CHUNK * j:CHUNK * j + CHUNK, 0:256 * (p + 1)], upper[p + 1][...], preferred_element_type=F32)

    def end_far(p, j, at, part):
        rest = kern[at, 128 * p:128 * p + 128] - halves(raw_far[j % 2, part, :])
        cross[at, :] = jnp.concatenate(split_two(rest), axis=1)

    def residual_of(j):
        both = jnp.concatenate(split_two(squares[CHUNK * j:CHUNK * j + CHUNK, :]), axis=1)
        spent = lax.dot_general(jnp.ones((8, 256), BF16), both, (((1,), (1,)), ((), ())), preferred_element_type=F32)
        for b in range(CHUNK // 128):
            row = j * (CHUNK // 128) + b
            own = amp_ref[row:row + 1, :]
            residual_ref[row:row + 1, :] = own * own - spent[0:1, 128 * b:128 * b + 128]

    def schedule(t):
        if 0 <= t < 16:
            start_first(t)
        if 1 <= t < 17:
            pending.extend(functools.partial(end_first, t - 1, *piece) for piece in pieces(t - 1))
        if 16 <= t < 80:
            start_near(t // 16 - 1, t % 16)
        if 18 <= t < 66:
            p, j = (t - 2) // 16 - 1, (t - 2) % 16
            pending.extend(functools.partial(end_far, p, j, *piece) for piece in pieces(j))
        if 17 <= t < 81:
            p, j = (t - 1) // 16 - 1, (t - 1) % 16
            pending.extend(functools.partial(end_near, p, j, *piece) for piece in pieces(j))
            if p < 3:
                pending.append(functools.partial(start_far, p, j))
        if 66 <= t < 82:
            pending.append(functools.partial(residual_of, t - 66))

    lane = lax.broadcasted_iota(jnp.int32, (128, 128), 1)
    sub = lax.broadcasted_iota(jnp.int32, (128, 128), 0)
    for p in range(4):
        lo = 128 * p

        def work(j):
            step(len(pending))
            if j < 15:
                schedule(16 * p + j + 1)
            if j >= 8 and later:
                pending.append(later.pop(0))

        schedule(16 * p)
        got = eliminate([matrix[lo + 8 * b:lo + 8 * b + 8, lo:lo + 128] for b in range(16)], work, step)
        inverse = jnp.where(lane <= sub, jnp.concatenate(got, axis=0), 0.0)
        inverse_t[p] = both_parts(inverse.T)
        parts = {}

        def extend(p, q, inverse, parts):
            part = jnp.dot(inverse, matrix[128 * p:128 * p + 128, 128 * q:128 * q + 128],
                           precision=HI, preferred_element_type=F32)
            parts[q] = part
            for r in range(p + 1, q + 1):
                matrix[128 * r:128 * r + 128, 128 * q:128 * q + 128] -= lax.dot_general(
                    parts[r], part, (((0,), (0,)), ((), ())), precision=HI, preferred_element_type=F32)
            upper[q][256 * p:256 * p + 256, :] = both_parts(part)

        if p < 3:
            extend(p, p + 1, inverse, parts)
        inverse_t[p] = both_parts(inverse.T)
        later.extend(functools.partial(extend, p, q, inverse, parts) for q in range(p + 2, 4))
    for t in range(64, 82):
        schedule(t)
        step(len(pending))
    return [tree(parts) for parts in sums]


SCRATCH = [
    pltpu.VMEM((512, 512), F32), pltpu.VMEM((256, 640), BF16), pltpu.VMEM((4096, 384), F32),
    pltpu.VMEM((4096, 256), BF16), pltpu.VMEM((4096, 768), BF16), pltpu.VMEM((4096, 128), F32),
    pltpu.VMEM((4, 256, 256), BF16),
    pltpu.VMEM((256, 256), BF16), pltpu.VMEM((512, 256), BF16), pltpu.VMEM((768, 256), BF16),
    pltpu.VMEM((2, CHUNK, 640), F32), pltpu.VMEM((2, CHUNK, 256), F32), pltpu.VMEM((2, CHUNK, 256), F32),
]


def far_first():
    found = [(min(y, 4 - y) + min(x, 4 - x) + min(z, 8 - z), y, x, z) for y in range(4) for x in range(4) for z in range(8)]
    return [offset[1:] for offset in sorted(found, key=lambda offset: -offset[0])][:-1]


FAR_FIRST = far_first()


def place():
    me = lax.axis_index("rows")
    core = lax.rem(me, 2)
    deep = lax.rem(me // 2, 8)
    plane = me // 16
    return me, core, deep, plane


def device_of(plane, deep, core):
    return (plane * 8 + deep) * 2 + core


def features_of(embed_ref, amp_ref, first):
    part = embed_ref[:, first:first + 128]
    amp = jnp.log2(amp_ref[first // 128:first // 128 + 1, :])
    squared = jnp.sum(part * part, axis=0, keepdims=True) * (LOG2E / 64)
    high, low = split_two(part)
    high, low = high.astype(F32), low.astype(F32)
    ones = jnp.ones((1, 128), F32)
    extra = [v.astype(F32) for v in split_three(squared)] + [ones] * 3 + [v.astype(F32) for v in split_three(amp)]
    row = lax.broadcasted_iota(jnp.int32, (64, 128), 0)
    tail = jnp.zeros((64, 128), F32)
    for index, value in enumerate(extra):
        tail = jnp.where(row == index, value, tail)
    one = jnp.concatenate([high, low], axis=0).T.astype(BF16)
    two = jnp.concatenate([high, tail], axis=0).T.astype(BF16)
    return one, two


def whole_kernel(points, pivots_hbm, embed_hbm, amp_hbm, factor_ref, residual_ref, means_ref,
                 pivots_ref, embed_ref, amp_ref, loaded, features_ref, chosen_ref,
                 own, column, whole, send1, recv1, send2, recv2, send3, recv3,
                 mine1, mine2, land2, total_sems,
                 matrix, pivots_t, kern, cross, done, squares, inverse_t, upper1, upper2, upper3,
                 raw_first, raw_near, raw_far):
    me, core, deep, plane = place()
    loads = [
        pltpu.make_async_copy(pivots_hbm, pivots_ref, loaded.at[0]),
        pltpu.make_async_copy(embed_hbm, embed_ref, loaded.at[1]),
        pltpu.make_async_copy(amp_hbm, amp_ref, loaded.at[2]),
    ]
    for load in loads:
        load.start()
    barrier = pltpu.get_barrier_semaphore()
    peers1 = [device_of(plane, lax.rem(deep + d, 8), core) for d in range(1, 8)]
    peers2 = [device_of(lax.rem(plane + d, 16), deep, core) for d in range(1, 16)]
    other = device_of(plane, deep, 1 - core)
    for peer in peers1 + peers2 + [other]:
        pl.semaphore_signal(barrier, inc=1, device_id=(peer,), device_id_type=MESH)

    for load in loads:
        load.wait()
    lane = lax.broadcasted_iota(jnp.int32, (4, 128), 1)
    pivots = pivots_ref[...]
    owners = pivots >> 12
    offsets = pivots & 4095
    mine = owners == me
    key = lane * 4096 + offsets
    first = jnp.min(jnp.where(mine, key, 128 * 4096 - 1), axis=1, keepdims=True) & 4095
    last = jnp.max(jnp.where(mine, key, 0), axis=1, keepdims=True) & 4095
    lanes = lax.broadcasted_iota(jnp.int32, (64, 128), 1)
    lanes2 = lax.broadcasted_iota(jnp.int32, (128, 128), 1)
    packed = jnp.zeros((128, 128), F32)
    for p in range(4):
        halves = []
        for found in (first, last):
            offset = jnp.broadcast_to(found[p:p + 1, 0:1], (64, 128))
            group = offset >> 7
            part = embed_ref[:, 0:128]
            for b in range(1, 32):
                part = jnp.where(group == b, embed_ref[:, 128 * b:128 * b + 128], part)
            halves.append(jnp.sum(jnp.where(lanes == (offset & 127), part, 0.0), axis=1, keepdims=True))
        packed = jnp.where(lanes2 == p, jnp.concatenate(halves, axis=0), packed)
    tile = packed.T[0:4, :]
    own[...] = tile
    column[deep] = tile

    pl.semaphore_wait(barrier, 23)

    copies1 = []
    for d in range(1, 8):
        copy = pltpu.make_async_remote_copy(
            src_ref=own, dst_ref=column.at[deep], send_sem=send1.at[d - 1], recv_sem=recv1.at[deep],
            device_id=(peers1[d - 1],), device_id_type=MESH)
        copy.start()
        copies1.append(copy)

    wanted = []
    sub2 = lax.broadcasted_iota(jnp.int32, (128, 128), 0)
    for p in range(4):
        row = jnp.broadcast_to(owners[p:p + 1, :], (128, 128)).astype(F32)
        col = row.T
        slot = jnp.sum(jnp.where((row == col) & (lanes2 < sub2), 1.0, 0.0), axis=1, keepdims=True)
        owner = col.astype(jnp.int32)
        spot = (owner & 1) * 128 + (owner >> 1)
        wanted.append((spot, slot))

    for start in range(0, 1024, 128):
        one, two = features_of(embed_ref, amp_ref, start)
        features_ref[start:start + 128, 0:128] = one
        features_ref[start:start + 128, 128:256] = two

    for d in range(1, 8):
        source = lax.rem(deep + d, 8)
        pltpu.make_async_remote_copy(
            src_ref=own, dst_ref=column.at[source], send_sem=send1.at[d - 1], recv_sem=recv1.at[source],
            device_id=(peers1[d - 1],), device_id_type=MESH).wait_recv()
    block = core * 16 + plane
    for p in range(4):
        whole[p, block] = jnp.concatenate([column[z][p:p + 1, :] for z in range(8)], axis=0)

    copies2 = []
    for d in range(1, 16):
        copy = pltpu.make_async_remote_copy(
            src_ref=whole.at[:, block], dst_ref=whole.at[:, block], send_sem=send2.at[d - 1], recv_sem=recv2.at[plane],
            device_id=(peers2[d - 1],), device_id_type=MESH)
        copy.start()
        copies2.append(copy)

    def forward(index, of_plane):
        at = core * 16 + of_plane
        copy = pltpu.make_async_remote_copy(
            src_ref=whole.at[:, at], dst_ref=whole.at[:, at], send_sem=send3.at[index], recv_sem=recv3.at[of_plane],
            device_id=(other,), device_id_type=MESH)
        copy.start()
        return copy

    copies3 = [forward(0, plane)]
    for start in range(1024, 4096, 128):
        one, two = features_of(embed_ref, amp_ref, start)
        features_ref[start:start + 128, 0:128] = one
        features_ref[start:start + 128, 128:256] = two

    for d in range(1, 16):
        source = lax.rem(plane + d, 16)
        at = core * 16 + source
        pltpu.make_async_remote_copy(
            src_ref=whole.at[:, at], dst_ref=whole.at[:, at], send_sem=send2.at[d - 1], recv_sem=recv2.at[source],
            device_id=(peers2[d - 1],), device_id_type=MESH).wait_recv()
        copies3.append(forward(d, source))
    for source in range(16):
        at = (1 - core) * 16 + source
        pltpu.make_async_remote_copy(
            src_ref=whole.at[:, at], dst_ref=whole.at[:, at], send_sem=send3.at[0], recv_sem=recv3.at[source],
            device_id=(other,), device_id_type=MESH).wait_recv()

    for p in range(4):
        spot, slot = wanted[p]
        rows = whole[p].reshape(256, 128)
        parts = jnp.concatenate(split_three(rows), axis=1)
        wide = lax.broadcasted_iota(jnp.int32, (128, 256), 1)
        take = jnp.where(wide == jnp.concatenate([spot, spot], axis=1), 1.0, 0.0).astype(BF16)
        got = jnp.dot(take, parts, preferred_element_type=F32)
        got = got[:, 0:128] + (got[:, 128:256] + got[:, 256:384])
        got = jnp.where(slot > 0.5, pltpu.roll(got, 64, 1), got)
        chosen_ref[128 * p:128 * p + 128, :] = jnp.where(lanes2 < 64, got, 0.0)

    for copy in copies1 + copies2 + copies3:
        copy.wait_send()

    later = prepare(chosen_ref, matrix, pivots_t)
    sums = factorise(features_ref, amp_ref, matrix, pivots_t, kern, cross, done, squares, inverse_t,
                     (None, upper1, upper2, upper3), raw_first, raw_near, raw_far, factor_ref, residual_ref, later)

    lane8 = lax.broadcasted_iota(jnp.int32, (8, 128), 1)
    total = jnp.sum(amp_ref[...] * amp_ref[...])
    value = jnp.zeros((8, 128), F32)
    for p in range(4):
        total = total - jnp.sum(sums[p])
        value = jnp.where(lane8 == p, total, value)

    mine1[core] = value
    copy = pltpu.make_async_remote_copy(
        src_ref=mine1.at[core], dst_ref=mine1.at[core], send_sem=total_sems.at[0], recv_sem=total_sems.at[1],
        device_id=(other,), device_id_type=MESH)
    copy.start()
    copy.wait_recv()
    chips = plane * 8 + deep
    mine2[...] = mine1[0, 0:1, :] + mine1[1, 0:1, :]
    land2[chips] = mine2[...]
    high, wide = plane // 4, lax.rem(plane, 4)
    targets = []
    for dy, dx, dz in FAR_FIRST:
        there = lax.rem(high + dy, 4) * 4 + lax.rem(wide + dx, 4)
        targets.append(device_of(there, lax.rem(deep + dz, 8), core))
    for target in targets:
        pltpu.make_async_remote_copy(
            src_ref=mine2, dst_ref=land2.at[chips], send_sem=total_sems.at[2], recv_sem=total_sems.at[3],
            device_id=(target,), device_id_type=MESH).start()
    every = pltpu.make_async_remote_copy(
        src_ref=land2.at[0:127], dst_ref=land2.at[0:127], send_sem=total_sems.at[2], recv_sem=total_sems.at[3],
        device_id=(targets[0],), device_id_type=MESH)
    every.wait_recv()
    means_ref[...] = jnp.sum(land2[...], axis=0)[:, 0:4] * (1.0 / points)
    copy.wait_send()
    every.wait_send()


def write_kernel(factor_ref, residual_ref, means_ref, factor_hbm, residual_hbm, means_hbm, sems):
    copies = [
        pltpu.make_async_copy(residual_ref, residual_hbm, sems.at[8]),
        pltpu.make_async_copy(means_ref, means_hbm, sems.at[9]),
    ]
    for part in range(8):
        rows = pl.ds(512 * part, 512)
        copies.append(pltpu.make_async_copy(factor_ref.at[rows], factor_hbm.at[rows], sems.at[part]))
    for copy in copies:
        copy.start()
    for copy in copies:
        copy.wait()


def local(embed, amplitude, pivots):
    points = 4096 * lax.axis_size("rows")
    factor, residual, means = pl.pallas_call(
        functools.partial(whole_kernel, points),
        out_shape=(jax.ShapeDtypeStruct((4096, 512), F32), jax.ShapeDtypeStruct((32, 128), F32),
                   jax.ShapeDtypeStruct((1, 4), F32)),
        in_specs=[pl.BlockSpec(memory_space=pltpu.HBM)] * 3,
        out_specs=[pl.BlockSpec(memory_space=pltpu.VMEM)] * 3,
        scratch_shapes=[
            pltpu.VMEM((4, 128), jnp.int32), pltpu.VMEM((64, 4096), F32), pltpu.VMEM((32, 128), F32),
            pltpu.SemaphoreType.DMA((3,)),
            pltpu.VMEM((4096, 256), BF16), pltpu.VMEM((512, 128), F32),
            pltpu.VMEM((4, 128), F32), pltpu.VMEM((8, 4, 128), F32), pltpu.VMEM((4, 32, 8, 128), F32),
            pltpu.SemaphoreType.DMA((7,)), pltpu.SemaphoreType.DMA((8,)),
            pltpu.SemaphoreType.DMA((15,)), pltpu.SemaphoreType.DMA((16,)),
            pltpu.SemaphoreType.DMA((16,)), pltpu.SemaphoreType.DMA((16,)),
            pltpu.VMEM((2, 8, 128), F32), pltpu.VMEM((1, 128), F32), pltpu.VMEM((128, 1, 128), F32),
            pltpu.SemaphoreType.DMA((4,)),
        ] + SCRATCH,
        compiler_params=pltpu.CompilerParams(collective_id=0, has_side_effects=True, vmem_limit_bytes=45000000),
        name="pivoted_cholesky",
    )(pivots, embed.T, amplitude.reshape(32, 128))
    factor, residual, means = pl.pallas_call(
        write_kernel,
        out_shape=(jax.ShapeDtypeStruct((4096, 512), F32), jax.ShapeDtypeStruct((32, 128), F32),
                   jax.ShapeDtypeStruct((1, 4), F32)),
        in_specs=[pl.BlockSpec(memory_space=pltpu.VMEM)] * 3,
        out_specs=[pl.BlockSpec(memory_space=pltpu.HBM)] * 3,
        scratch_shapes=[pltpu.SemaphoreType.DMA((10,))],
        compiler_params=pltpu.CompilerParams(vmem_limit_bytes=1 << 20),
        name="write_out",
    )(factor, residual, means)
    return factor, residual.reshape(4096), means.reshape(4)


def solution(mesh):
    return jax.shard_map(
        local,
        mesh=mesh,
        in_specs=(P("rows", None), P("rows"), P()),
        out_specs=(P("rows", None), P("rows"), P()),
        check_vma=False,
    )
```

```python
import functools

import jax
import jax.numpy as jnp
from jax import lax
from jax.experimental import pallas as pl
from jax.experimental.pallas import tpu as pltpu
from jax.sharding import PartitionSpec as P

HI = lax.Precision.HIGHEST
F32 = jnp.float32

LOG2E = 1.4426950408889634
MESH = pl.DeviceIdType.MESH
BF16 = jnp.bfloat16


def spread_row(block, row):
    return jnp.broadcast_to(block[row:row + 1, :], (8, 128))


def spread_col(block, col):
    return jnp.broadcast_to(block[:, col:col + 1], (8, 128))


def tree(terms):
    while len(terms) > 1:
        terms = [a + b for a, b in zip(terms[::2], terms[1::2])] + ([terms[-1]] if len(terms) % 2 else [])
    return terms[0]


def eliminate_rows(blocks, base, work, step):
    lane = lax.broadcasted_iota(jnp.int32, (8, 128), 1)
    sub = lax.broadcasted_iota(jnp.int32, (8, 128), 0)
    count = len(blocks)
    blocks = list(blocks)
    diag = [spread_col(blocks[0], base + k) for k in range(8)]
    for j in range(count):
        at = base + 8 * j
        inside = (lane >= at) & (lane < at + 8)
        below = {b: [spread_col(blocks[b], at + k) for k in range(8)] for b in range(j + 1, count)}
        following = [spread_col(blocks[j + 1], at + 8 + k) for k in range(8)] if j + 1 < count else None
        rest = jnp.where(inside, jnp.where(lane - at == sub, 1.0, 0.0), blocks[j])
        rows = []
        for k in range(8):
            scale = lax.rsqrt(spread_row(diag[k], k))
            low = diag[k] * scale
            row = spread_row(rest, k) * scale
            rows.append(row)
            if k < 7:
                rest = rest - low * row
            for b in below:
                below[b][k] = below[b][k] * scale
            for m in range(k + 1, 8):
                factor = spread_row(low, m)
                diag[m] = diag[m] - low * factor
                for b in below:
                    below[b][m] = below[b][m] - below[b][k] * factor
            step()
        out = rows[0]
        for k in range(1, 8):
            out = jnp.where(sub == k, rows[k], out)
        blocks[j] = out
        if j + 1 < count:
            first = below[j + 1]
            diag = [following[k] - tree([first[m] * spread_row(first[m], k) for m in range(8)]) for k in range(8)]
        for b in below:
            blocks[b] = jnp.where(inside, 0.0, blocks[b]) - tree([below[b][k] * rows[k] for k in range(8)])
        work(at // 8)
    return blocks


def eliminate(blocks, work, step, width=64):
    lane = lax.broadcasted_iota(jnp.int32, (8, 128), 1)
    blocks = list(blocks)
    group = width // 8
    for base in range(0, 128, width):
        first = base // 8
        blocks[first:first + group] = eliminate_rows(blocks[first:first + group], base, work, step)
        if base + width < 128:
            rows = jnp.concatenate(blocks[first:first + group], axis=0)
            row = lax.broadcasted_iota(jnp.int32, (width, 128), 0) + base
            col = lax.broadcasted_iota(jnp.int32, (width, 128), 1)
            lower = jnp.where((col > row) & (col < base + width), 0.0, rows)
            change = lax.dot_general(rows, lower, (((0,), (0,)), ((), ())), precision=HI, preferred_element_type=F32)
            inside = (lane >= base) & (lane < base + width)
            for b in range(first + group, 16):
                blocks[b] = jnp.where(inside, 0.0, blocks[b]) - change[8 * b:8 * b + 8, :]
    return blocks


def split_two(value):
    high = value.astype(BF16)
    return high, (value - high.astype(F32)).astype(BF16)


def split_three(value):
    high = value.astype(BF16)
    left = value - high.astype(F32)
    middle = left.astype(BF16)
    return high, middle, (left - middle.astype(F32)).astype(BF16)


def both_parts(value):
    both = jnp.concatenate(split_two(value), axis=1)
    return jnp.concatenate([both, both], axis=0)


def halves(value):
    return value[:, 0:128] + value[:, 128:256]


def prepare(chosen_ref, matrix, pivots_t):
    lane = lax.broadcasted_iota(jnp.int32, (128, 128), 1)
    lefts, rights = [], []

    def beside(first, second):
        return jnp.where(lane < 64, first, pltpu.roll(second, 64, 1))

    def with_tail(first, values):
        out = jnp.where(lane < 64, first, 0.0)
        for index, value in enumerate(values):
            out = jnp.where(lane == 64 + index, value, out)
        return out

    def block(p, q, size):
        right = jnp.concatenate(rights[q:q + size], axis=0)
        power = lax.dot_general(lefts[p], right, (((1,), (1,)), ((), ())), preferred_element_type=F32)
        matrix[128 * p:128 * p + 128, 128 * q:128 * (q + size)] = jnp.exp2(jnp.minimum(power, 0.0))

    for p in range(4):
        at = slice(128 * p, 128 * p + 128)
        chosen = chosen_ref[at, :]
        squared = jnp.sum(chosen * chosen, axis=1, keepdims=True) * (LOG2E / 64)
        squares = [part.astype(F32) for part in split_three(squared)]
        high, middle, low = [part.astype(F32) for part in split_three(chosen)]
        left = [beside(high, middle), with_tail(high, squares + [1.0] * 3), beside(middle, high), with_tail(low, [])]
        lefts.append(jnp.concatenate([part.astype(BF16) for part in left], axis=1))
        high, middle, low = [part.astype(F32) for part in split_three(chosen * (2 * LOG2E / 64))]
        one = beside(high, high)
        two = with_tail(middle, [-1.0] * 3 + [-part for part in squares] + [1.0] * 3)
        right = [one, two, beside(middle, low), with_tail(high, [])]
        rights.append(jnp.concatenate([part.astype(BF16) for part in right], axis=1))
        if p == 0:
            block(0, 0, 1)
        pivots_t[0:128, at] = one.T.astype(BF16)
        pivots_t[128:256, at] = two.T.astype(BF16)
    row = lax.broadcasted_iota(jnp.int32, (256, 128), 0)
    pivots_t[:, 512:640] = jnp.where((row >= 198) & (row < 201), 1.0, 0.0).astype(BF16)
    return [functools.partial(block, *which) for which in ((0, 1, 3), (1, 1, 3), (2, 2, 2), (3, 3, 1))]


CHUNK = 256
CHUNKS = 4096 // CHUNK
PIECE = 32
PER_STEP = 2


def factorise(features_ref, amp_ref, matrix, pivots_t, kern, cross, done, squares, inverse_t, upper,
              raw_first, raw_near, raw_far, factor_ref, residual_ref, later):
    sums = [[] for _ in range(4)]
    pending = []

    def step(count=PER_STEP):
        for _ in range(min(count, len(pending))):
            pending.pop(0)()

    def pieces(j):
        return [(slice(CHUNK * j + r, CHUNK * j + r + PIECE), slice(r, r + PIECE)) for r in range(0, CHUNK, PIECE)]

    def start_first(j):
        raw_first[j % 2] = jnp.dot(
            features_ref[CHUNK * j:CHUNK * j + CHUNK, :], pivots_t[...], preferred_element_type=F32)

    def end_first(j, at, part):
        top = raw_first[j % 2, part, 512:640]
        near = [jnp.exp2(jnp.minimum(raw_first[j % 2, part, 128 * q:128 * q + 128], top)) for q in range(4)]
        cross[at, :] = jnp.concatenate(split_two(near[0]), axis=1)
        kern[at, :] = jnp.concatenate(near[1:], axis=1)

    def start_near(p, j):
        raw_near[j % 2] = jnp.dot(
            cross[CHUNK * j:CHUNK * j + CHUNK, :], inverse_t[p], preferred_element_type=F32)

    def end_near(p, j, at, part):
        got = halves(raw_near[j % 2, part, :])
        factor_ref[at, 128 * p:128 * p + 128] = got
        square = got * got
        sums[p].append(tree([square[8 * b:8 * b + 8, :] for b in range(PIECE // 8)]))
        if p < 3:
            squares[at, :] = square if p == 0 else squares[at, :] + square
            done[at, 256 * p:256 * p + 256] = jnp.concatenate(split_two(got), axis=1)
        else:
            squares[at, :] = squares[at, :] + square

    def start_far(p, j):
        raw_far[j % 2] = jnp.dot(
            done[CHUNK * j:CHUNK * j + CHUNK, 0:256 * (p + 1)], upper[p + 1][...], preferred_element_type=F32)

    def end_far(p, j, at, part):
        rest = kern[at, 128 * p:128 * p + 128] - halves(raw_far[j % 2, part, :])
        cross[at, :] = jnp.concatenate(split_two(rest), axis=1)

    def residual_of(j):
        both = jnp.concatenate(split_two(squares[CHUNK * j:CHUNK * j + CHUNK, :]), axis=1)
        spent = lax.dot_general(jnp.ones((8, 256), BF16), both, (((1,), (1,)), ((), ())), preferred_element_type=F32)
        for b in range(CHUNK // 128):
            row = j * (CHUNK // 128) + b
            own = amp_ref[row:row + 1, :]
            residual_ref[row:row + 1, :] = own * own - spent[0:1, 128 * b:128 * b + 128]

    def schedule(t):
        if 0 <= t < 16:
            start_first(t)
        if 1 <= t < 17:
            pending.extend(functools.partial(end_first, t - 1, *piece) for piece in pieces(t - 1))
        if 16 <= t < 80:
            start_near(t // 16 - 1, t % 16)
        if 18 <= t < 66:
            p, j = (t - 2) // 16 - 1, (t - 2) % 16
            pending.extend(functools.partial(end_far, p, j, *piece) for piece in pieces(j))
        if 17 <= t < 81:
            p, j = (t - 1) // 16 - 1, (t - 1) % 16
            pending.extend(functools.partial(end_near, p, j, *piece) for piece in pieces(j))
            if p < 3:
                pending.append(functools.partial(start_far, p, j))
        if 66 <= t < 82:
            pending.append(functools.partial(residual_of, t - 66))

    lane = lax.broadcasted_iota(jnp.int32, (128, 128), 1)
    sub = lax.broadcasted_iota(jnp.int32, (128, 128), 0)
    for p in range(4):
        lo = 128 * p

        def work(j):
            step(len(pending))
            if j < 15:
                schedule(16 * p + j + 1)
            if j >= 8 and later:
                pending.append(later.pop(0))

        schedule(16 * p)
        got = eliminate([matrix[lo + 8 * b:lo + 8 * b + 8, lo:lo + 128] for b in range(16)], work, step)
        inverse = jnp.where(lane <= sub, jnp.concatenate(got, axis=0), 0.0)
        inverse_t[p] = both_parts(inverse.T)
        parts = {}

        def extend(p, q, inverse, parts):
            part = jnp.dot(inverse, matrix[128 * p:128 * p + 128, 128 * q:128 * q + 128],
                           precision=HI, preferred_element_type=F32)
            parts[q] = part
            for r in range(p + 1, q + 1):
                matrix[128 * r:128 * r + 128, 128 * q:128 * q + 128] -= lax.dot_general(
                    parts[r], part, (((0,), (0,)), ((), ())), precision=HI, preferred_element_type=F32)
            upper[q][256 * p:256 * p + 256, :] = both_parts(part)

        if p < 3:
            extend(p, p + 1, inverse, parts)
        inverse_t[p] = both_parts(inverse.T)
        later.extend(functools.partial(extend, p, q, inverse, parts) for q in range(p + 2, 4))
    for t in range(64, 82):
        schedule(t)
        step(len(pending))
    return [tree(parts) for parts in sums]


SCRATCH = [
    pltpu.VMEM((512, 512), F32), pltpu.VMEM((256, 640), BF16), pltpu.VMEM((4096, 384), F32),
    pltpu.VMEM((4096, 256), BF16), pltpu.VMEM((4096, 768), BF16), pltpu.VMEM((4096, 128), F32),
    pltpu.VMEM((4, 256, 256), BF16),
    pltpu.VMEM((256, 256), BF16), pltpu.VMEM((512, 256), BF16), pltpu.VMEM((768, 256), BF16),
    pltpu.VMEM((2, CHUNK, 640), F32), pltpu.VMEM((2, CHUNK, 256), F32), pltpu.VMEM((2, CHUNK, 256), F32),
]


def far_first():
    found = [
        (min(y, 4 - y) + min(x, 4 - x) + min(z, 8 - z), y, x, z, c)
        for y in range(4) for x in range(4) for z in range(8) for c in range(2)
    ]
    return [offset[1:] for offset in sorted(found, key=lambda offset: (-offset[0], -offset[4]))][:-1]


FAR_FIRST = far_first()


def place():
    me = lax.axis_index("rows")
    core = lax.rem(me, 2)
    deep = lax.rem(me // 2, 8)
    plane = me // 16
    return me, core, deep, plane


def device_of(plane, deep, core):
    return (plane * 8 + deep) * 2 + core


def features_of(embed_ref, amp_ref, first):
    part = embed_ref[:, first:first + 128]
    amp = jnp.log2(amp_ref[first // 128:first // 128 + 1, :])
    squared = jnp.sum(part * part, axis=0, keepdims=True) * (LOG2E / 64)
    high, low = split_two(part)
    high, low = high.astype(F32), low.astype(F32)
    ones = jnp.ones((1, 128), F32)
    extra = [v.astype(F32) for v in split_three(squared)] + [ones] * 3 + [v.astype(F32) for v in split_three(amp)]
    row = lax.broadcasted_iota(jnp.int32, (64, 128), 0)
    tail = jnp.zeros((64, 128), F32)
    for index, value in enumerate(extra):
        tail = jnp.where(row == index, value, tail)
    one = jnp.concatenate([high, low], axis=0).T.astype(BF16)
    two = jnp.concatenate([high, tail], axis=0).T.astype(BF16)
    return one, two


def whole_kernel(points, pivots_hbm, embed_hbm, amp_hbm, factor_ref, residual_ref, means_ref,
                 pivots_ref, embed_ref, amp_ref, loaded, features_ref, chosen_ref,
                 own, column, whole, send1, recv1, send2, recv2, send3, recv3,
                 my_sums, all_sums, total_sems,
                 matrix, pivots_t, kern, cross, done, squares, inverse_t, upper1, upper2, upper3,
                 raw_first, raw_near, raw_far):
    me, core, deep, plane = place()
    loads = [
        pltpu.make_async_copy(pivots_hbm, pivots_ref, loaded.at[0]),
        pltpu.make_async_copy(embed_hbm, embed_ref, loaded.at[1]),
        pltpu.make_async_copy(amp_hbm, amp_ref, loaded.at[2]),
    ]
    for load in loads:
        load.start()
    barrier = pltpu.get_barrier_semaphore()
    peers1 = [device_of(plane, lax.rem(deep + d, 8), core) for d in range(1, 8)]
    peers2 = [device_of(lax.rem(plane + d, 16), deep, core) for d in range(1, 16)]
    other = device_of(plane, deep, 1 - core)
    for peer in peers1 + peers2 + [other]:
        pl.semaphore_signal(barrier, inc=1, device_id=(peer,), device_id_type=MESH)

    for load in loads:
        load.wait()
    lane = lax.broadcasted_iota(jnp.int32, (4, 128), 1)
    pivots = pivots_ref[...]
    owners = pivots >> 12
    offsets = pivots & 4095
    mine = owners == me
    key = lane * 4096 + offsets
    first = jnp.min(jnp.where(mine, key, 128 * 4096 - 1), axis=1, keepdims=True) & 4095
    last = jnp.max(jnp.where(mine, key, 0), axis=1, keepdims=True) & 4095
    lanes = lax.broadcasted_iota(jnp.int32, (64, 128), 1)
    lanes2 = lax.broadcasted_iota(jnp.int32, (128, 128), 1)
    packed = jnp.zeros((128, 128), F32)
    for p in range(4):
        halves = []
        for found in (first, last):
            offset = jnp.broadcast_to(found[p:p + 1, 0:1], (64, 128))
            group = offset >> 7
            part = embed_ref[:, 0:128]
            for b in range(1, 32):
                part = jnp.where(group == b, embed_ref[:, 128 * b:128 * b + 128], part)
            halves.append(jnp.sum(jnp.where(lanes == (offset & 127), part, 0.0), axis=1, keepdims=True))
        packed = jnp.where(lanes2 == p, jnp.concatenate(halves, axis=0), packed)
    tile = packed.T[0:4, :]
    own[...] = tile
    column[deep] = tile

    pl.semaphore_wait(barrier, 23)

    copies1 = []
    for d in range(1, 8):
        copy = pltpu.make_async_remote_copy(
            src_ref=own, dst_ref=column.at[deep], send_sem=send1.at[d - 1], recv_sem=recv1.at[deep],
            device_id=(peers1[d - 1],), device_id_type=MESH)
        copy.start()
        copies1.append(copy)

    wanted = []
    sub2 = lax.broadcasted_iota(jnp.int32, (128, 128), 0)
    for p in range(4):
        row = jnp.broadcast_to(owners[p:p + 1, :], (128, 128)).astype(F32)
        col = row.T
        slot = jnp.sum(jnp.where((row == col) & (lanes2 < sub2), 1.0, 0.0), axis=1, keepdims=True)
        owner = col.astype(jnp.int32)
        spot = (owner & 1) * 128 + (owner >> 1)
        wanted.append((spot, slot))

    for start in range(0, 1024, 128):
        one, two = features_of(embed_ref, amp_ref, start)
        features_ref[start:start + 128, 0:128] = one
        features_ref[start:start + 128, 128:256] = two

    for d in range(1, 8):
        source = lax.rem(deep + d, 8)
        pltpu.make_async_remote_copy(
            src_ref=own, dst_ref=column.at[source], send_sem=send1.at[d - 1], recv_sem=recv1.at[source],
            device_id=(peers1[d - 1],), device_id_type=MESH).wait_recv()
    block = core * 16 + plane
    for p in range(4):
        whole[p, block] = jnp.concatenate([column[z][p:p + 1, :] for z in range(8)], axis=0)

    copies2 = []
    for d in range(1, 16):
        copy = pltpu.make_async_remote_copy(
            src_ref=whole.at[:, block], dst_ref=whole.at[:, block], send_sem=send2.at[d - 1], recv_sem=recv2.at[plane],
            device_id=(peers2[d - 1],), device_id_type=MESH)
        copy.start()
        copies2.append(copy)

    def forward(index, of_plane):
        at = core * 16 + of_plane
        copy = pltpu.make_async_remote_copy(
            src_ref=whole.at[:, at], dst_ref=whole.at[:, at], send_sem=send3.at[index], recv_sem=recv3.at[of_plane],
            device_id=(other,), device_id_type=MESH)
        copy.start()
        return copy

    copies3 = [forward(0, plane)]
    for start in range(1024, 4096, 128):
        one, two = features_of(embed_ref, amp_ref, start)
        features_ref[start:start + 128, 0:128] = one
        features_ref[start:start + 128, 128:256] = two

    for d in range(1, 16):
        source = lax.rem(plane + d, 16)
        at = core * 16 + source
        pltpu.make_async_remote_copy(
            src_ref=whole.at[:, at], dst_ref=whole.at[:, at], send_sem=send2.at[d - 1], recv_sem=recv2.at[source],
            device_id=(peers2[d - 1],), device_id_type=MESH).wait_recv()
        copies3.append(forward(d, source))
    for source in range(16):
        at = (1 - core) * 16 + source
        pltpu.make_async_remote_copy(
            src_ref=whole.at[:, at], dst_ref=whole.at[:, at], send_sem=send3.at[0], recv_sem=recv3.at[source],
            device_id=(other,), device_id_type=MESH).wait_recv()

    for p in range(4):
        spot, slot = wanted[p]
        rows = whole[p].reshape(256, 128)
        parts = jnp.concatenate(split_three(rows), axis=1)
        wide = lax.broadcasted_iota(jnp.int32, (128, 256), 1)
        take = jnp.where(wide == jnp.concatenate([spot, spot], axis=1), 1.0, 0.0).astype(BF16)
        got = jnp.dot(take, parts, preferred_element_type=F32)
        got = got[:, 0:128] + (got[:, 128:256] + got[:, 256:384])
        got = jnp.where(slot > 0.5, pltpu.roll(got, 64, 1), got)
        chosen_ref[128 * p:128 * p + 128, :] = jnp.where(lanes2 < 64, got, 0.0)

    for copy in copies1 + copies2 + copies3:
        copy.wait_send()

    later = prepare(chosen_ref, matrix, pivots_t)
    sums = factorise(features_ref, amp_ref, matrix, pivots_t, kern, cross, done, squares, inverse_t,
                     (None, upper1, upper2, upper3), raw_first, raw_near, raw_far, factor_ref, residual_ref, later)

    lane8 = lax.broadcasted_iota(jnp.int32, (8, 128), 1)
    total = jnp.sum(amp_ref[...] * amp_ref[...])
    value = jnp.zeros((8, 128), F32)
    for p in range(4):
        total = total - jnp.sum(sums[p])
        value = jnp.where(lane8 == p, total, value)

    my_sums[...] = value[0:1, :]
    all_sums[me] = my_sums[...]
    high, wide = plane // 4, lax.rem(plane, 4)
    targets = []
    for dy, dx, dz, dc in FAR_FIRST:
        there = lax.rem(high + dy, 4) * 4 + lax.rem(wide + dx, 4)
        targets.append(device_of(there, lax.rem(deep + dz, 8), lax.rem(core + dc, 2)))
    for target in targets:
        pltpu.make_async_remote_copy(
            src_ref=my_sums, dst_ref=all_sums.at[me], send_sem=total_sems.at[0], recv_sem=total_sems.at[1],
            device_id=(target,), device_id_type=MESH).start()
    every = pltpu.make_async_remote_copy(
        src_ref=all_sums.at[0:255], dst_ref=all_sums.at[0:255], send_sem=total_sems.at[0], recv_sem=total_sems.at[1],
        device_id=(targets[0],), device_id_type=MESH)
    every.wait_recv()
    means_ref[...] = jnp.sum(all_sums[...], axis=0)[:, 0:4] * (1.0 / points)
    every.wait_send()


def write_kernel(factor_ref, residual_ref, means_ref, factor_hbm, residual_hbm, means_hbm, sems):
    copies = [
        pltpu.make_async_copy(residual_ref, residual_hbm, sems.at[8]),
        pltpu.make_async_copy(means_ref, means_hbm, sems.at[9]),
    ]
    for part in range(8):
        rows = pl.ds(512 * part, 512)
        copies.append(pltpu.make_async_copy(factor_ref.at[rows], factor_hbm.at[rows], sems.at[part]))
    for copy in copies:
        copy.start()
    for copy in copies:
        copy.wait()


def local(embed, amplitude, pivots):
    points = 4096 * lax.axis_size("rows")
    operands = [
        pltpu.with_memory_space_constraint(value, pltpu.HBM)
        for value in (pivots, embed.T, amplitude.reshape(32, 128))
    ]
    factor, residual, means = pl.pallas_call(
        functools.partial(whole_kernel, points),
        out_shape=(jax.ShapeDtypeStruct((4096, 512), F32), jax.ShapeDtypeStruct((32, 128), F32),
                   jax.ShapeDtypeStruct((1, 4), F32)),
        in_specs=[pl.BlockSpec(memory_space=pltpu.HBM)] * 3,
        out_specs=[pl.BlockSpec(memory_space=pltpu.VMEM)] * 3,
        scratch_shapes=[
            pltpu.VMEM((4, 128), jnp.int32), pltpu.VMEM((64, 4096), F32), pltpu.VMEM((32, 128), F32),
            pltpu.SemaphoreType.DMA((3,)),
            pltpu.VMEM((4096, 256), BF16), pltpu.VMEM((512, 128), F32),
            pltpu.VMEM((4, 128), F32), pltpu.VMEM((8, 4, 128), F32), pltpu.VMEM((4, 32, 8, 128), F32),
            pltpu.SemaphoreType.DMA((7,)), pltpu.SemaphoreType.DMA((8,)),
            pltpu.SemaphoreType.DMA((15,)), pltpu.SemaphoreType.DMA((16,)),
            pltpu.SemaphoreType.DMA((16,)), pltpu.SemaphoreType.DMA((16,)),
            pltpu.VMEM((1, 128), F32), pltpu.VMEM((256, 1, 128), F32), pltpu.SemaphoreType.DMA((2,)),
        ] + SCRATCH,
        compiler_params=pltpu.CompilerParams(collective_id=0, has_side_effects=True, vmem_limit_bytes=45000000),
        name="pivoted_cholesky",
    )(*operands)
    factor, residual, means = pl.pallas_call(
        write_kernel,
        out_shape=(jax.ShapeDtypeStruct((4096, 512), F32), jax.ShapeDtypeStruct((32, 128), F32),
                   jax.ShapeDtypeStruct((1, 4), F32)),
        in_specs=[pl.BlockSpec(memory_space=pltpu.VMEM)] * 3,
        out_specs=[pl.BlockSpec(memory_space=pltpu.HBM)] * 3,
        scratch_shapes=[pltpu.SemaphoreType.DMA((10,))],
        compiler_params=pltpu.CompilerParams(vmem_limit_bytes=1 << 20),
        name="write_out",
    )(factor, residual, means)
    return factor, residual.reshape(4096), means.reshape(4)


def solution(mesh):
    return jax.shard_map(
        local,
        mesh=mesh,
        in_specs=(P("rows", None), P("rows"), P()),
        out_specs=(P("rows", None), P("rows"), P()),
        check_vma=False,
    )
```

```python
import functools

import jax
import jax.numpy as jnp
from jax import lax
from jax.experimental import pallas as pl
from jax.experimental.pallas import tpu as pltpu
from jax.sharding import PartitionSpec as P

HI = lax.Precision.HIGHEST
F32 = jnp.float32

LOG2E = 1.4426950408889634
MESH = pl.DeviceIdType.MESH
BF16 = jnp.bfloat16


def spread_row(block, row):
    return jnp.broadcast_to(block[row:row + 1, :], (8, 128))


def spread_col(block, col):
    return jnp.broadcast_to(block[:, col:col + 1], (8, 128))


def tree(terms):
    while len(terms) > 1:
        terms = [a + b for a, b in zip(terms[::2], terms[1::2])] + ([terms[-1]] if len(terms) % 2 else [])
    return terms[0]


def eliminate_rows(blocks, base, work, step):
    lane = lax.broadcasted_iota(jnp.int32, (8, 128), 1)
    sub = lax.broadcasted_iota(jnp.int32, (8, 128), 0)
    count = len(blocks)
    blocks = list(blocks)
    diag = [spread_col(blocks[0], base + k) for k in range(8)]
    for j in range(count):
        at = base + 8 * j
        inside = (lane >= at) & (lane < at + 8)
        below = {b: [spread_col(blocks[b], at + k) for k in range(8)] for b in range(j + 1, count)}
        following = [spread_col(blocks[j + 1], at + 8 + k) for k in range(8)] if j + 1 < count else None
        rest = jnp.where(inside, jnp.where(lane - at == sub, 1.0, 0.0), blocks[j])
        rows = []
        for k in range(8):
            scale = lax.rsqrt(spread_row(diag[k], k))
            low = diag[k] * scale
            row = spread_row(rest, k) * scale
            rows.append(row)
            if k < 7:
                rest = rest - low * row
            for b in below:
                below[b][k] = below[b][k] * scale
            for m in range(k + 1, 8):
                factor = spread_row(low, m)
                diag[m] = diag[m] - low * factor
                for b in below:
                    below[b][m] = below[b][m] - below[b][k] * factor
            step()
        out = rows[0]
        for k in range(1, 8):
            out = jnp.where(sub == k, rows[k], out)
        blocks[j] = out
        if j + 1 < count:
            first = below[j + 1]
            diag = [following[k] - tree([first[m] * spread_row(first[m], k) for m in range(8)]) for k in range(8)]
        for b in below:
            blocks[b] = jnp.where(inside, 0.0, blocks[b]) - tree([below[b][k] * rows[k] for k in range(8)])
        work(at // 8)
    return blocks


def eliminate(blocks, work, step, width=64):
    lane = lax.broadcasted_iota(jnp.int32, (8, 128), 1)
    blocks = list(blocks)
    group = width // 8
    for base in range(0, 128, width):
        first = base // 8
        blocks[first:first + group] = eliminate_rows(blocks[first:first + group], base, work, step)
        if base + width < 128:
            rows = jnp.concatenate(blocks[first:first + group], axis=0)
            row = lax.broadcasted_iota(jnp.int32, (width, 128), 0) + base
            col = lax.broadcasted_iota(jnp.int32, (width, 128), 1)
            lower = jnp.where((col > row) & (col < base + width), 0.0, rows)
            change = lax.dot_general(rows, lower, (((0,), (0,)), ((), ())), precision=HI, preferred_element_type=F32)
            inside = (lane >= base) & (lane < base + width)
            for b in range(first + group, 16):
                blocks[b] = jnp.where(inside, 0.0, blocks[b]) - change[8 * b:8 * b + 8, :]
    return blocks


def split_two(value):
    high = value.astype(BF16)
    return high, (value - high.astype(F32)).astype(BF16)


def split_three(value):
    high = value.astype(BF16)
    left = value - high.astype(F32)
    middle = left.astype(BF16)
    return high, middle, (left - middle.astype(F32)).astype(BF16)


def both_parts(value):
    both = jnp.concatenate(split_two(value), axis=1)
    return jnp.concatenate([both, both], axis=0)


def halves(value):
    return value[:, 0:128] + value[:, 128:256]


def prepare(pick, matrix, pivots_t):
    lane = lax.broadcasted_iota(jnp.int32, (128, 128), 1)
    lefts, rights = [], []

    def beside(first, second):
        return jnp.where(lane < 64, first, pltpu.roll(second, 64, 1))

    def with_tail(first, values):
        out = jnp.where(lane < 64, first, 0.0)
        for index, value in enumerate(values):
            out = jnp.where(lane == 64 + index, value, out)
        return out

    def block(p, q, size):
        right = jnp.concatenate(rights[q:q + size], axis=0)
        power = lax.dot_general(lefts[p], right, (((1,), (1,)), ((), ())), preferred_element_type=F32)
        matrix[128 * p:128 * p + 128, 128 * q:128 * (q + size)] = jnp.exp2(jnp.minimum(power, 0.0))

    for p in range(4):
        at = slice(128 * p, 128 * p + 128)
        chosen = pick(p)
        squared = jnp.sum(chosen * chosen, axis=1, keepdims=True) * (LOG2E / 64)
        squares = [part.astype(F32) for part in split_three(squared)]
        high, middle, low = [part.astype(F32) for part in split_three(chosen)]
        left = [beside(high, middle), with_tail(high, squares + [1.0] * 3), beside(middle, high), with_tail(low, [])]
        lefts.append(jnp.concatenate([part.astype(BF16) for part in left], axis=1))
        high, middle, low = [part.astype(F32) for part in split_three(chosen * (2 * LOG2E / 64))]
        one = beside(high, high)
        two = with_tail(middle, [-1.0] * 3 + [-part for part in squares] + [1.0] * 3)
        right = [one, two, beside(middle, low), with_tail(high, [])]
        rights.append(jnp.concatenate([part.astype(BF16) for part in right], axis=1))
        if p == 0:
            block(0, 0, 1)
        pivots_t[0:128, at] = one.T.astype(BF16)
        pivots_t[128:256, at] = two.T.astype(BF16)
    row = lax.broadcasted_iota(jnp.int32, (256, 128), 0)
    pivots_t[:, 512:640] = jnp.where((row >= 198) & (row < 201), 1.0, 0.0).astype(BF16)
    return [functools.partial(block, *which) for which in ((0, 1, 3), (1, 1, 3), (2, 2, 2), (3, 3, 1))]


CHUNK = 256
CHUNKS = 4096 // CHUNK
PIECE = 32
PER_STEP = 2


def factorise(features_ref, amp_ref, matrix, pivots_t, kern, cross, done, squares, inverse_t, upper,
              raw_first, raw_near, raw_far, factor_ref, later):
    sums = [[] for _ in range(4)]
    pending = []

    def step(count=PER_STEP):
        for _ in range(min(count, len(pending))):
            pending.pop(0)()

    def pieces(j):
        return [(slice(CHUNK * j + r, CHUNK * j + r + PIECE), slice(r, r + PIECE)) for r in range(0, CHUNK, PIECE)]

    def start_first(j):
        raw_first[j % 2] = jnp.dot(
            features_ref[CHUNK * j:CHUNK * j + CHUNK, :], pivots_t[...], preferred_element_type=F32)

    def end_first(j, at, part):
        top = raw_first[j % 2, part, 512:640]
        near = [jnp.exp2(jnp.minimum(raw_first[j % 2, part, 128 * q:128 * q + 128], top)) for q in range(4)]
        cross[at, :] = jnp.concatenate(split_two(near[0]), axis=1)
        kern[at, :] = jnp.concatenate(near[1:], axis=1)

    def start_near(p, j):
        raw_near[j % 2] = jnp.dot(
            cross[CHUNK * j:CHUNK * j + CHUNK, :], inverse_t[p], preferred_element_type=F32)

    def end_near(p, j, at, part):
        got = halves(raw_near[j % 2, part, :])
        factor_ref[at, 128 * p:128 * p + 128] = got
        square = got * got
        sums[p].append(tree([square[8 * b:8 * b + 8, :] for b in range(PIECE // 8)]))
        if p < 3:
            squares[at, :] = square if p == 0 else squares[at, :] + square
            done[at, 256 * p:256 * p + 256] = jnp.concatenate(split_two(got), axis=1)

    def start_far(p, j):
        raw_far[j % 2] = jnp.dot(
            done[CHUNK * j:CHUNK * j + CHUNK, 0:256 * (p + 1)], upper[p + 1][...], preferred_element_type=F32)

    def end_far(p, j, at, part):
        rest = kern[at, 128 * p:128 * p + 128] - halves(raw_far[j % 2, part, :])
        cross[at, :] = jnp.concatenate(split_two(rest), axis=1)

    def schedule(t):
        if 0 <= t < 16:
            start_first(t)
        if 1 <= t < 17:
            pending.extend(functools.partial(end_first, t - 1, *piece) for piece in pieces(t - 1))
        if 16 <= t < 80:
            start_near(t // 16 - 1, t % 16)
        if 18 <= t < 66:
            p, j = (t - 2) // 16 - 1, (t - 2) % 16
            pending.extend(functools.partial(end_far, p, j, *piece) for piece in pieces(j))
        if 17 <= t < 81:
            p, j = (t - 1) // 16 - 1, (t - 1) % 16
            pending.extend(functools.partial(end_near, p, j, *piece) for piece in pieces(j))
            if p < 3:
                pending.append(functools.partial(start_far, p, j))

    lane = lax.broadcasted_iota(jnp.int32, (128, 128), 1)
    sub = lax.broadcasted_iota(jnp.int32, (128, 128), 0)
    for p in range(4):
        lo = 128 * p

        def work(j):
            step(len(pending))
            if j < 15:
                schedule(16 * p + j + 1)
            if j >= 8 and later:
                pending.append(later.pop(0))

        schedule(16 * p)
        got = eliminate([matrix[lo + 8 * b:lo + 8 * b + 8, lo:lo + 128] for b in range(16)], work, step)
        inverse = jnp.where(lane <= sub, jnp.concatenate(got, axis=0), 0.0)
        inverse_t[p] = both_parts(inverse.T)
        parts = {}

        def extend(p, q, inverse, parts):
            part = jnp.dot(inverse, matrix[128 * p:128 * p + 128, 128 * q:128 * q + 128],
                           precision=HI, preferred_element_type=F32)
            parts[q] = part
            for r in range(p + 1, q + 1):
                matrix[128 * r:128 * r + 128, 128 * q:128 * q + 128] -= lax.dot_general(
                    parts[r], part, (((0,), (0,)), ((), ())), precision=HI, preferred_element_type=F32)
            upper[q][256 * p:256 * p + 256, :] = both_parts(part)

        if p < 3:
            extend(p, p + 1, inverse, parts)
        inverse_t[p] = both_parts(inverse.T)
        later.extend(functools.partial(extend, p, q, inverse, parts) for q in range(p + 2, 4))
    for t in range(64, 81):
        schedule(t)
        step(len(pending))
    return [tree(parts) for parts in sums]


def residuals(amp_ref, squares, factor_ref, residual_ref):
    for j in range(CHUNKS):
        at = slice(CHUNK * j, CHUNK * j + CHUNK)
        last = factor_ref[at, 384:512]
        both = jnp.concatenate(split_two(squares[at, :] + last * last), axis=1)
        spent = lax.dot_general(jnp.ones((8, 256), BF16), both, (((1,), (1,)), ((), ())), preferred_element_type=F32)
        for b in range(CHUNK // 128):
            row = j * (CHUNK // 128) + b
            own = amp_ref[row:row + 1, :]
            residual_ref[row:row + 1, :] = own * own - spent[0:1, 128 * b:128 * b + 128]


SCRATCH = [
    pltpu.VMEM((512, 512), F32), pltpu.VMEM((256, 640), BF16), pltpu.VMEM((4096, 384), F32),
    pltpu.VMEM((4096, 256), BF16), pltpu.VMEM((4096, 768), BF16), pltpu.VMEM((4096, 128), F32),
    pltpu.VMEM((4, 256, 256), BF16),
    pltpu.VMEM((256, 256), BF16), pltpu.VMEM((512, 256), BF16), pltpu.VMEM((768, 256), BF16),
    pltpu.VMEM((2, CHUNK, 640), F32), pltpu.VMEM((2, CHUNK, 256), F32), pltpu.VMEM((2, CHUNK, 256), F32),
]


def far_first():
    found = [
        (min(y, 4 - y) + min(x, 4 - x) + min(z, 8 - z), y, x, z, c)
        for y in range(4) for x in range(4) for z in range(8) for c in range(2)
    ]
    return [offset[1:] for offset in sorted(found, key=lambda offset: (-offset[0], -offset[4]))][:-1]


FAR_FIRST = far_first()


def place():
    me = lax.axis_index("rows")
    core = lax.rem(me, 2)
    deep = lax.rem(me // 2, 8)
    plane = me // 16
    return me, core, deep, plane


def device_of(plane, deep, core):
    return (plane * 8 + deep) * 2 + core


def features_of(embed_ref, amp_ref, first):
    part = embed_ref[:, first:first + 128]
    amp = jnp.log2(amp_ref[first // 128:first // 128 + 1, :])
    squared = jnp.sum(part * part, axis=0, keepdims=True) * (LOG2E / 64)
    high, low = split_two(part)
    high, low = high.astype(F32), low.astype(F32)
    ones = jnp.ones((1, 128), F32)
    extra = [v.astype(F32) for v in split_three(squared)] + [ones] * 3 + [v.astype(F32) for v in split_three(amp)]
    row = lax.broadcasted_iota(jnp.int32, (64, 128), 0)
    tail = jnp.zeros((64, 128), F32)
    for index, value in enumerate(extra):
        tail = jnp.where(row == index, value, tail)
    one = jnp.concatenate([high, low], axis=0).T.astype(BF16)
    two = jnp.concatenate([high, tail], axis=0).T.astype(BF16)
    return one, two


def whole_kernel(points, pivots_hbm, embed_hbm, amp_hbm, factor_ref, residual_ref, means_ref,
                 pivots_ref, embed_ref, amp_ref, loaded, features_ref,
                 own, column, whole, send1, recv1, send2, recv2, send3, recv3,
                 my_sums, all_sums, total_sems,
                 matrix, pivots_t, kern, cross, done, squares, inverse_t, upper1, upper2, upper3,
                 raw_first, raw_near, raw_far):
    me, core, deep, plane = place()
    loads = [
        pltpu.make_async_copy(pivots_hbm, pivots_ref, loaded.at[0]),
        pltpu.make_async_copy(embed_hbm, embed_ref, loaded.at[1]),
        pltpu.make_async_copy(amp_hbm, amp_ref, loaded.at[2]),
    ]
    for load in loads:
        load.start()
    barrier = pltpu.get_barrier_semaphore()
    peers1 = [device_of(plane, lax.rem(deep + d, 8), core) for d in range(1, 8)]
    peers2 = [device_of(lax.rem(plane + d, 16), deep, core) for d in range(1, 16)]
    other = device_of(plane, deep, 1 - core)
    for peer in peers1 + peers2 + [other]:
        pl.semaphore_signal(barrier, inc=1, device_id=(peer,), device_id_type=MESH)

    for load in loads:
        load.wait()
    lane = lax.broadcasted_iota(jnp.int32, (4, 128), 1)
    pivots = pivots_ref[...]
    owners = pivots >> 12
    offsets = pivots & 4095
    mine = owners == me
    key = lane * 4096 + offsets
    first = jnp.min(jnp.where(mine, key, 128 * 4096 - 1), axis=1, keepdims=True) & 4095
    last = jnp.max(jnp.where(mine, key, 0), axis=1, keepdims=True) & 4095
    lanes = lax.broadcasted_iota(jnp.int32, (64, 128), 1)
    lanes2 = lax.broadcasted_iota(jnp.int32, (128, 128), 1)
    packed = jnp.zeros((128, 128), F32)
    for p in range(4):
        halves = []
        for found in (first, last):
            offset = jnp.broadcast_to(found[p:p + 1, 0:1], (64, 128))
            group = offset >> 7
            part = embed_ref[:, 0:128]
            for b in range(1, 32):
                part = jnp.where(group == b, embed_ref[:, 128 * b:128 * b + 128], part)
            halves.append(jnp.sum(jnp.where(lanes == (offset & 127), part, 0.0), axis=1, keepdims=True))
        packed = jnp.where(lanes2 == p, jnp.concatenate(halves, axis=0), packed)
    tile = packed.T[0:4, :]
    own[...] = tile
    column[deep] = tile

    pl.semaphore_wait(barrier, 23)

    copies1 = []
    for d in range(1, 8):
        copy = pltpu.make_async_remote_copy(
            src_ref=own, dst_ref=column.at[deep], send_sem=send1.at[d - 1], recv_sem=recv1.at[deep],
            device_id=(peers1[d - 1],), device_id_type=MESH)
        copy.start()
        copies1.append(copy)

    wanted = []
    sub2 = lax.broadcasted_iota(jnp.int32, (128, 128), 0)
    for p in range(4):
        row = jnp.broadcast_to(owners[p:p + 1, :], (128, 128)).astype(F32)
        col = row.T
        slot = jnp.sum(jnp.where((row == col) & (lanes2 < sub2), 1.0, 0.0), axis=1, keepdims=True)
        owner = col.astype(jnp.int32)
        spot = (owner & 1) * 128 + (owner >> 1)
        wanted.append((spot, slot))

    for start in range(0, 1024, 128):
        one, two = features_of(embed_ref, amp_ref, start)
        features_ref[start:start + 128, 0:128] = one
        features_ref[start:start + 128, 128:256] = two

    for d in range(1, 8):
        source = lax.rem(deep + d, 8)
        pltpu.make_async_remote_copy(
            src_ref=own, dst_ref=column.at[source], send_sem=send1.at[d - 1], recv_sem=recv1.at[source],
            device_id=(peers1[d - 1],), device_id_type=MESH).wait_recv()
    block = core * 16 + plane
    for p in range(4):
        whole[p, block] = jnp.concatenate([column[z][p:p + 1, :] for z in range(8)], axis=0)

    copies2 = []
    for d in range(1, 16):
        copy = pltpu.make_async_remote_copy(
            src_ref=whole.at[:, block], dst_ref=whole.at[:, block], send_sem=send2.at[d - 1], recv_sem=recv2.at[plane],
            device_id=(peers2[d - 1],), device_id_type=MESH)
        copy.start()
        copies2.append(copy)

    def forward(index, of_plane):
        at = core * 16 + of_plane
        copy = pltpu.make_async_remote_copy(
            src_ref=whole.at[:, at], dst_ref=whole.at[:, at], send_sem=send3.at[index], recv_sem=recv3.at[of_plane],
            device_id=(other,), device_id_type=MESH)
        copy.start()
        return copy

    copies3 = [forward(0, plane)]
    for start in range(1024, 4096, 128):
        one, two = features_of(embed_ref, amp_ref, start)
        features_ref[start:start + 128, 0:128] = one
        features_ref[start:start + 128, 128:256] = two

    for d in range(1, 16):
        source = lax.rem(plane + d, 16)
        at = core * 16 + source
        pltpu.make_async_remote_copy(
            src_ref=whole.at[:, at], dst_ref=whole.at[:, at], send_sem=send2.at[d - 1], recv_sem=recv2.at[source],
            device_id=(peers2[d - 1],), device_id_type=MESH).wait_recv()
        copies3.append(forward(d, source))
    for source in range(16):
        at = (1 - core) * 16 + source
        pltpu.make_async_remote_copy(
            src_ref=whole.at[:, at], dst_ref=whole.at[:, at], send_sem=send3.at[0], recv_sem=recv3.at[source],
            device_id=(other,), device_id_type=MESH).wait_recv()

    def pick(p):
        spot, slot = wanted[p]
        rows = whole[p].reshape(256, 128)
        parts = jnp.concatenate(split_three(rows), axis=1)
        wide = lax.broadcasted_iota(jnp.int32, (128, 256), 1)
        take = jnp.where(wide == jnp.concatenate([spot, spot], axis=1), 1.0, 0.0).astype(BF16)
        got = jnp.dot(take, parts, preferred_element_type=F32)
        got = got[:, 0:128] + (got[:, 128:256] + got[:, 256:384])
        got = jnp.where(slot > 0.5, pltpu.roll(got, 64, 1), got)
        return jnp.where(lanes2 < 64, got, 0.0)

    later = prepare(pick, matrix, pivots_t)
    sums = factorise(features_ref, amp_ref, matrix, pivots_t, kern, cross, done, squares, inverse_t,
                     (None, upper1, upper2, upper3), raw_first, raw_near, raw_far, factor_ref, later)

    lane8 = lax.broadcasted_iota(jnp.int32, (8, 128), 1)
    own_squares = amp_ref[...] * amp_ref[...]
    total = tree([own_squares[8 * b:8 * b + 8, :] for b in range(4)])
    value = jnp.zeros((8, 128), F32)
    for p in range(4):
        total = total - sums[p]
        value = jnp.where(lane8 == p, jnp.sum(jnp.sum(total, axis=0, keepdims=True), axis=1, keepdims=True), value)

    my_sums[...] = value[0:1, :]
    all_sums[me] = my_sums[...]
    high, wide = plane // 4, lax.rem(plane, 4)
    targets = []
    for dy, dx, dz, dc in FAR_FIRST:
        there = lax.rem(high + dy, 4) * 4 + lax.rem(wide + dx, 4)
        targets.append(device_of(there, lax.rem(deep + dz, 8), lax.rem(core + dc, 2)))
    for target in targets:
        pltpu.make_async_remote_copy(
            src_ref=my_sums, dst_ref=all_sums.at[me], send_sem=total_sems.at[0], recv_sem=total_sems.at[1],
            device_id=(target,), device_id_type=MESH).start()
    every = pltpu.make_async_remote_copy(
        src_ref=all_sums.at[0:255], dst_ref=all_sums.at[0:255], send_sem=total_sems.at[0], recv_sem=total_sems.at[1],
        device_id=(targets[0],), device_id_type=MESH)
    residuals(amp_ref, squares, factor_ref, residual_ref)
    every.wait_recv()
    means_ref[...] = jnp.sum(all_sums[...], axis=0)[:, 0:4] * (1.0 / points)
    every.wait_send()
    for copy in copies1 + copies2 + copies3:
        copy.wait_send()


def write_kernel(factor_ref, residual_ref, means_ref, factor_hbm, residual_hbm, means_hbm, sems):
    copies = [
        pltpu.make_async_copy(residual_ref, residual_hbm, sems.at[8]),
        pltpu.make_async_copy(means_ref, means_hbm, sems.at[9]),
    ]
    for part in range(8):
        rows = pl.ds(512 * part, 512)
        copies.append(pltpu.make_async_copy(factor_ref.at[rows], factor_hbm.at[rows], sems.at[part]))
    for copy in copies:
        copy.start()
    for copy in copies:
        copy.wait()


def local(embed, amplitude, pivots):
    points = 4096 * lax.axis_size("rows")
    operands = [
        pltpu.with_memory_space_constraint(value, pltpu.HBM)
        for value in (pivots, embed.T, amplitude.reshape(32, 128))
    ]
    factor, residual, means = pl.pallas_call(
        functools.partial(whole_kernel, points),
        out_shape=(jax.ShapeDtypeStruct((4096, 512), F32), jax.ShapeDtypeStruct((32, 128), F32),
                   jax.ShapeDtypeStruct((1, 4), F32)),
        in_specs=[pl.BlockSpec(memory_space=pltpu.HBM)] * 3,
        out_specs=[pl.BlockSpec(memory_space=pltpu.VMEM)] * 3,
        scratch_shapes=[
            pltpu.VMEM((4, 128), jnp.int32), pltpu.VMEM((64, 4096), F32), pltpu.VMEM((32, 128), F32),
            pltpu.SemaphoreType.DMA((3,)),
            pltpu.VMEM((4096, 256), BF16),
            pltpu.VMEM((4, 128), F32), pltpu.VMEM((8, 4, 128), F32), pltpu.VMEM((4, 32, 8, 128), F32),
            pltpu.SemaphoreType.DMA((7,)), pltpu.SemaphoreType.DMA((8,)),
            pltpu.SemaphoreType.DMA((15,)), pltpu.SemaphoreType.DMA((16,)),
            pltpu.SemaphoreType.DMA((16,)), pltpu.SemaphoreType.DMA((16,)),
            pltpu.VMEM((1, 128), F32), pltpu.VMEM((256, 1, 128), F32), pltpu.SemaphoreType.DMA((2,)),
        ] + SCRATCH,
        compiler_params=pltpu.CompilerParams(collective_id=0, has_side_effects=True, vmem_limit_bytes=45000000),
        name="pivoted_cholesky",
    )(*operands)
    factor, residual, means = pl.pallas_call(
        write_kernel,
        out_shape=(jax.ShapeDtypeStruct((4096, 512), F32), jax.ShapeDtypeStruct((32, 128), F32),
                   jax.ShapeDtypeStruct((1, 4), F32)),
        in_specs=[pl.BlockSpec(memory_space=pltpu.VMEM)] * 3,
        out_specs=[pl.BlockSpec(memory_space=pltpu.HBM)] * 3,
        scratch_shapes=[pltpu.SemaphoreType.DMA((10,))],
        compiler_params=pltpu.CompilerParams(vmem_limit_bytes=1 << 20),
        name="write_out",
    )(factor, residual, means)
    return factor, residual.reshape(4096), means.reshape(4)


def solution(mesh):
    return jax.shard_map(
        local,
        mesh=mesh,
        in_specs=(P("rows", None), P("rows"), P()),
        out_specs=(P("rows", None), P("rows"), P()),
        check_vma=False,
    )
```

```python
import functools

import jax
import jax.numpy as jnp
from jax import lax
from jax.experimental import pallas as pl
from jax.experimental.pallas import tpu as pltpu
from jax.sharding import PartitionSpec as P

HI = lax.Precision.HIGHEST
F32 = jnp.float32

LOG2E = 1.4426950408889634
MESH = pl.DeviceIdType.MESH
BF16 = jnp.bfloat16


def spread_row(block, row):
    return jnp.broadcast_to(block[row:row + 1, :], (8, 128))


def spread_col(block, col):
    return jnp.broadcast_to(block[:, col:col + 1], (8, 128))


def tree(terms):
    while len(terms) > 1:
        terms = [a + b for a, b in zip(terms[::2], terms[1::2])] + ([terms[-1]] if len(terms) % 2 else [])
    return terms[0]


def eliminate_rows(blocks, base, work, step):
    lane = lax.broadcasted_iota(jnp.int32, (8, 128), 1)
    sub = lax.broadcasted_iota(jnp.int32, (8, 128), 0)
    count = len(blocks)
    blocks = list(blocks)
    diag = [spread_col(blocks[0], base + k) for k in range(8)]
    for j in range(count):
        at = base + 8 * j
        inside = (lane >= at) & (lane < at + 8)
        below = {b: [spread_col(blocks[b], at + k) for k in range(8)] for b in range(j + 1, count)}
        following = [spread_col(blocks[j + 1], at + 8 + k) for k in range(8)] if j + 1 < count else None
        rest = jnp.where(inside, jnp.where(lane - at == sub, 1.0, 0.0), blocks[j])
        rows = []
        for k in range(8):
            scale = lax.rsqrt(spread_row(diag[k], k))
            low = diag[k] * scale
            row = spread_row(rest, k) * scale
            rows.append(row)
            if k < 7:
                rest = rest - low * row
            for b in below:
                below[b][k] = below[b][k] * scale
            for m in range(k + 1, 8):
                factor = spread_row(low, m)
                diag[m] = diag[m] - low * factor
                for b in below:
                    below[b][m] = below[b][m] - below[b][k] * factor
            step()
        out = rows[0]
        for k in range(1, 8):
            out = jnp.where(sub == k, rows[k], out)
        blocks[j] = out
        if j + 1 < count:
            first = below[j + 1]
            diag = [following[k] - tree([first[m] * spread_row(first[m], k) for m in range(8)]) for k in range(8)]
        for b in below:
            blocks[b] = jnp.where(inside, 0.0, blocks[b]) - tree([below[b][k] * rows[k] for k in range(8)])
        work(at // 8)
    return blocks


def eliminate(blocks, work, step, width=64):
    lane = lax.broadcasted_iota(jnp.int32, (8, 128), 1)
    blocks = list(blocks)
    group = width // 8
    for base in range(0, 128, width):
        first = base // 8
        blocks[first:first + group] = eliminate_rows(blocks[first:first + group], base, work, step)
        if base + width < 128:
            rows = jnp.concatenate(blocks[first:first + group], axis=0)
            row = lax.broadcasted_iota(jnp.int32, (width, 128), 0) + base
            col = lax.broadcasted_iota(jnp.int32, (width, 128), 1)
            lower = jnp.where((col > row) & (col < base + width), 0.0, rows)
            change = lax.dot_general(rows, lower, (((0,), (0,)), ((), ())), precision=HI, preferred_element_type=F32)
            inside = (lane >= base) & (lane < base + width)
            for b in range(first + group, 16):
                blocks[b] = jnp.where(inside, 0.0, blocks[b]) - change[8 * b:8 * b + 8, :]
    return blocks


def split_two(value):
    high = value.astype(BF16)
    return high, (value - high.astype(F32)).astype(BF16)


def split_three(value):
    high = value.astype(BF16)
    left = value - high.astype(F32)
    middle = left.astype(BF16)
    return high, middle, (left - middle.astype(F32)).astype(BF16)


def both_parts(value):
    both = jnp.concatenate(split_two(value), axis=1)
    return jnp.concatenate([both, both], axis=0)


def halves(value):
    return value[:, 0:128] + value[:, 128:256]


def prepare(pick, matrix, pivots_t):
    lane = lax.broadcasted_iota(jnp.int32, (128, 128), 1)
    lefts, rights = [], []

    def beside(first, second):
        return jnp.where(lane < 64, first, pltpu.roll(second, 64, 1))

    def with_tail(first, values):
        out = jnp.where(lane < 64, first, 0.0)
        for index, value in enumerate(values):
            out = jnp.where(lane == 64 + index, value, out)
        return out

    def block(p, q, size):
        right = jnp.concatenate(rights[q:q + size], axis=0)
        power = lax.dot_general(lefts[p], right, (((1,), (1,)), ((), ())), preferred_element_type=F32)
        matrix[128 * p:128 * p + 128, 128 * q:128 * (q + size)] = jnp.exp2(jnp.minimum(power, 0.0))

    for p in range(4):
        at = slice(128 * p, 128 * p + 128)
        chosen = pick(p)
        squared = jnp.sum(chosen * chosen, axis=1, keepdims=True) * (LOG2E / 64)
        squares = [part.astype(F32) for part in split_three(squared)]
        high, middle, low = [part.astype(F32) for part in split_three(chosen)]
        left = [beside(high, middle), with_tail(high, squares + [1.0] * 3), beside(middle, high), with_tail(low, [])]
        lefts.append(jnp.concatenate([part.astype(BF16) for part in left], axis=1))
        high, middle, low = [part.astype(F32) for part in split_three(chosen * (2 * LOG2E / 64))]
        one = beside(high, high)
        two = with_tail(middle, [-1.0] * 3 + [-part for part in squares] + [1.0] * 3)
        right = [one, two, beside(middle, low), with_tail(high, [])]
        rights.append(jnp.concatenate([part.astype(BF16) for part in right], axis=1))
        if p == 0:
            block(0, 0, 1)
        pivots_t[0:128, at] = one.T.astype(BF16)
        pivots_t[128:256, at] = two.T.astype(BF16)
    row = lax.broadcasted_iota(jnp.int32, (256, 128), 0)
    pivots_t[:, 512:640] = jnp.where((row >= 198) & (row < 201), 1.0, 0.0).astype(BF16)
    return [functools.partial(block, *which) for which in ((0, 1, 3), (1, 1, 3), (2, 2, 2), (3, 3, 1))]


CHUNK = 256
CHUNKS = 4096 // CHUNK
PIECE = 32
PER_STEP = 2


def factorise(features_ref, amp_ref, matrix, pivots_t, kern, cross, done, squares, inverse_t, upper,
              raw_first, raw_near, raw_far, factor_ref, later):
    sums = [[] for _ in range(4)]
    pending = []

    def step(count=PER_STEP):
        for _ in range(min(count, len(pending))):
            pending.pop(0)()

    def pieces(j):
        return [(slice(CHUNK * j + r, CHUNK * j + r + PIECE), slice(r, r + PIECE)) for r in range(0, CHUNK, PIECE)]

    def start_first(j):
        raw_first[j % 2] = jnp.dot(
            features_ref[CHUNK * j:CHUNK * j + CHUNK, :], pivots_t[...], preferred_element_type=F32)

    def end_first(j, at, part):
        top = raw_first[j % 2, part, 512:640]
        near = [jnp.exp2(jnp.minimum(raw_first[j % 2, part, 128 * q:128 * q + 128], top)) for q in range(4)]
        cross[at, :] = jnp.concatenate(split_two(near[0]), axis=1)
        kern[at, :] = jnp.concatenate(near[1:], axis=1)

    def start_near(p, j):
        raw_near[j % 2] = jnp.dot(
            cross[CHUNK * j:CHUNK * j + CHUNK, :], inverse_t[p], preferred_element_type=F32)

    def end_near(p, j, at, part):
        got = halves(raw_near[j % 2, part, :])
        factor_ref[at, 128 * p:128 * p + 128] = got
        square = got * got
        sums[p].append(tree([square[8 * b:8 * b + 8, :] for b in range(PIECE // 8)]))
        if p < 3:
            squares[at, :] = square if p == 0 else squares[at, :] + square
            done[at, 256 * p:256 * p + 256] = jnp.concatenate(split_two(got), axis=1)

    def start_far(p, j):
        raw_far[j % 2] = jnp.dot(
            done[CHUNK * j:CHUNK * j + CHUNK, 0:256 * (p + 1)], upper[p + 1][...], preferred_element_type=F32)

    def end_far(p, j, at, part):
        rest = kern[at, 128 * p:128 * p + 128] - halves(raw_far[j % 2, part, :])
        cross[at, :] = jnp.concatenate(split_two(rest), axis=1)

    def schedule(t):
        if 0 <= t < 16:
            start_first(t)
        if 1 <= t < 17:
            pending.extend(functools.partial(end_first, t - 1, *piece) for piece in pieces(t - 1))
        if 16 <= t < 80:
            start_near(t // 16 - 1, t % 16)
        if 18 <= t < 66:
            p, j = (t - 2) // 16 - 1, (t - 2) % 16
            pending.extend(functools.partial(end_far, p, j, *piece) for piece in pieces(j))
        if 17 <= t < 81:
            p, j = (t - 1) // 16 - 1, (t - 1) % 16
            pending.extend(functools.partial(end_near, p, j, *piece) for piece in pieces(j))
            if p < 3:
                pending.append(functools.partial(start_far, p, j))

    lane = lax.broadcasted_iota(jnp.int32, (128, 128), 1)
    sub = lax.broadcasted_iota(jnp.int32, (128, 128), 0)
    for p in range(4):
        lo = 128 * p

        def work(j):
            step(len(pending))
            if j < 15:
                schedule(16 * p + j + 1)
            if j >= 8 and later:
                pending.append(later.pop(0))

        schedule(16 * p)
        got = eliminate([matrix[lo + 8 * b:lo + 8 * b + 8, lo:lo + 128] for b in range(16)], work, step)
        inverse = jnp.where(lane <= sub, jnp.concatenate(got, axis=0), 0.0)
        inverse_t[p] = both_parts(inverse.T)
        parts = {}

        def extend(p, q, inverse, parts):
            part = jnp.dot(inverse, matrix[128 * p:128 * p + 128, 128 * q:128 * q + 128],
                           precision=HI, preferred_element_type=F32)
            parts[q] = part
            for r in range(p + 1, q + 1):
                matrix[128 * r:128 * r + 128, 128 * q:128 * q + 128] -= lax.dot_general(
                    parts[r], part, (((0,), (0,)), ((), ())), precision=HI, preferred_element_type=F32)
            upper[q][256 * p:256 * p + 256, :] = both_parts(part)

        if p < 3:
            extend(p, p + 1, inverse, parts)
        inverse_t[p] = both_parts(inverse.T)
        later.extend(functools.partial(extend, p, q, inverse, parts) for q in range(p + 2, 4))
    for t in range(64, 81):
        schedule(t)
        step(len(pending))
    return [tree(parts) for parts in sums]


def residuals(amp_ref, squares, factor_ref, residual_ref):
    for j in range(CHUNKS):
        at = slice(CHUNK * j, CHUNK * j + CHUNK)
        last = factor_ref[at, 384:512]
        both = jnp.concatenate(split_two(squares[at, :] + last * last), axis=1)
        spent = lax.dot_general(jnp.ones((8, 256), BF16), both, (((1,), (1,)), ((), ())), preferred_element_type=F32)
        for b in range(CHUNK // 128):
            row = j * (CHUNK // 128) + b
            own = amp_ref[row:row + 1, :]
            residual_ref[row:row + 1, :] = own * own - spent[0:1, 128 * b:128 * b + 128]


SCRATCH = [
    pltpu.VMEM((512, 512), F32), pltpu.VMEM((256, 640), BF16), pltpu.VMEM((4096, 384), F32),
    pltpu.VMEM((4096, 256), BF16), pltpu.VMEM((4096, 768), BF16), pltpu.VMEM((4096, 128), F32),
    pltpu.VMEM((4, 256, 256), BF16),
    pltpu.VMEM((256, 256), BF16), pltpu.VMEM((512, 256), BF16), pltpu.VMEM((768, 256), BF16),
    pltpu.VMEM((2, CHUNK, 640), F32), pltpu.VMEM((2, CHUNK, 256), F32), pltpu.VMEM((2, CHUNK, 256), F32),
]


def far_first():
    found = [
        (min(y, 4 - y) + min(x, 4 - x) + min(z, 8 - z), y, x, z, c)
        for y in range(4) for x in range(4) for z in range(8) for c in range(2)
    ]
    return [offset[1:] for offset in sorted(found, key=lambda offset: (-offset[0], -offset[4]))][:-1]


FAR_FIRST = far_first()
PLANES_FAR_FIRST = [(dy, dx) for dy, dx, dz, dc in FAR_FIRST if dz == 0 and dc == 0]


def place():
    me = lax.axis_index("rows")
    core = lax.rem(me, 2)
    deep = lax.rem(me // 2, 8)
    plane = me // 16
    return me, core, deep, plane


def device_of(plane, deep, core):
    return (plane * 8 + deep) * 2 + core


def features_of(embed_ref, amp_ref, first):
    part = embed_ref[:, first:first + 128]
    amp = jnp.log2(amp_ref[first // 128:first // 128 + 1, :])
    squared = jnp.sum(part * part, axis=0, keepdims=True) * (LOG2E / 64)
    high, low = split_two(part)
    high, low = high.astype(F32), low.astype(F32)
    ones = jnp.ones((1, 128), F32)
    extra = [v.astype(F32) for v in split_three(squared)] + [ones] * 3 + [v.astype(F32) for v in split_three(amp)]
    row = lax.broadcasted_iota(jnp.int32, (64, 128), 0)
    tail = jnp.zeros((64, 128), F32)
    for index, value in enumerate(extra):
        tail = jnp.where(row == index, value, tail)
    one = jnp.concatenate([high, low], axis=0).T.astype(BF16)
    two = jnp.concatenate([high, tail], axis=0).T.astype(BF16)
    return one, two


def whole_kernel(points, pivots_hbm, embed_hbm, amp_hbm, factor_ref, residual_ref, means_ref,
                 pivots_ref, embed_ref, amp_ref, loaded, features_ref,
                 own, column, whole, send1, recv1, send2, recv2, send3, recv3,
                 my_sums, all_sums, total_sems,
                 matrix, pivots_t, kern, cross, done, squares, inverse_t, upper1, upper2, upper3,
                 raw_first, raw_near, raw_far):
    me, core, deep, plane = place()
    loads = [
        pltpu.make_async_copy(pivots_hbm, pivots_ref, loaded.at[0]),
        pltpu.make_async_copy(embed_hbm, embed_ref, loaded.at[1]),
        pltpu.make_async_copy(amp_hbm, amp_ref, loaded.at[2]),
    ]
    for load in loads:
        load.start()
    barrier = pltpu.get_barrier_semaphore()
    peers1 = [device_of(plane, lax.rem(deep + d, 8), core) for d in range(1, 8)]
    turn = lambda dy, dx: lax.rem(plane // 4 + dy, 4) * 4 + lax.rem(lax.rem(plane, 4) + dx, 4)
    planes = [turn(dy, dx) for dy, dx in PLANES_FAR_FIRST]
    peers2 = [device_of(there, deep, core) for there in planes]
    other = device_of(plane, deep, 1 - core)
    for peer in peers1 + peers2 + [other]:
        pl.semaphore_signal(barrier, inc=1, device_id=(peer,), device_id_type=MESH)

    for load in loads:
        load.wait()
    lane = lax.broadcasted_iota(jnp.int32, (4, 128), 1)
    pivots = pivots_ref[...]
    owners = pivots >> 12
    offsets = pivots & 4095
    mine = owners == me
    key = lane * 4096 + offsets
    first = jnp.min(jnp.where(mine, key, 128 * 4096 - 1), axis=1, keepdims=True) & 4095
    last = jnp.max(jnp.where(mine, key, 0), axis=1, keepdims=True) & 4095
    lanes = lax.broadcasted_iota(jnp.int32, (64, 128), 1)
    lanes2 = lax.broadcasted_iota(jnp.int32, (128, 128), 1)
    packed = jnp.zeros((128, 128), F32)
    for p in range(4):
        halves = []
        for found in (first, last):
            offset = jnp.broadcast_to(found[p:p + 1, 0:1], (64, 128))
            group = offset >> 7
            part = embed_ref[:, 0:128]
            for b in range(1, 32):
                part = jnp.where(group == b, embed_ref[:, 128 * b:128 * b + 128], part)
            halves.append(jnp.sum(jnp.where(lanes == (offset & 127), part, 0.0), axis=1, keepdims=True))
        packed = jnp.where(lanes2 == p, jnp.concatenate(halves, axis=0), packed)
    tile = packed.T[0:4, :]
    own[...] = tile
    column[deep] = tile

    pl.semaphore_wait(barrier, 23)

    copies1 = []
    for d in (4, 3, 5, 2, 6, 1, 7):
        copy = pltpu.make_async_remote_copy(
            src_ref=own, dst_ref=column.at[deep], send_sem=send1.at[d - 1], recv_sem=recv1.at[deep],
            device_id=(peers1[d - 1],), device_id_type=MESH)
        copy.start()
        copies1.append(copy)

    wanted = []
    sub2 = lax.broadcasted_iota(jnp.int32, (128, 128), 0)
    for p in range(4):
        row = jnp.broadcast_to(owners[p:p + 1, :], (128, 128)).astype(F32)
        col = row.T
        slot = jnp.sum(jnp.where((row == col) & (lanes2 < sub2), 1.0, 0.0), axis=1, keepdims=True)
        owner = col.astype(jnp.int32)
        spot = (owner & 1) * 128 + (owner >> 1)
        wanted.append((spot, slot))

    for start in range(0, 1024, 128):
        one, two = features_of(embed_ref, amp_ref, start)
        features_ref[start:start + 128, 0:128] = one
        features_ref[start:start + 128, 128:256] = two

    for d in range(1, 8):
        source = lax.rem(deep + d, 8)
        pltpu.make_async_remote_copy(
            src_ref=own, dst_ref=column.at[source], send_sem=send1.at[d - 1], recv_sem=recv1.at[source],
            device_id=(peers1[d - 1],), device_id_type=MESH).wait_recv()
    block = core * 16 + plane
    for p in range(4):
        whole[p, block] = jnp.concatenate([column[z][p:p + 1, :] for z in range(8)], axis=0)

    copies2 = []
    for d in range(1, 16):
        copy = pltpu.make_async_remote_copy(
            src_ref=whole.at[:, block], dst_ref=whole.at[:, block], send_sem=send2.at[d - 1], recv_sem=recv2.at[plane],
            device_id=(peers2[d - 1],), device_id_type=MESH)
        copy.start()
        copies2.append(copy)

    def forward(index, of_plane):
        at = core * 16 + of_plane
        copy = pltpu.make_async_remote_copy(
            src_ref=whole.at[:, at], dst_ref=whole.at[:, at], send_sem=send3.at[index], recv_sem=recv3.at[of_plane],
            device_id=(other,), device_id_type=MESH)
        copy.start()
        return copy

    copies3 = [forward(0, plane)]
    for start in range(1024, 4096, 128):
        one, two = features_of(embed_ref, amp_ref, start)
        features_ref[start:start + 128, 0:128] = one
        features_ref[start:start + 128, 128:256] = two

    for d in range(15, 0, -1):
        source = planes[d - 1]
        at = core * 16 + source
        pltpu.make_async_remote_copy(
            src_ref=whole.at[:, at], dst_ref=whole.at[:, at], send_sem=send2.at[d - 1], recv_sem=recv2.at[source],
            device_id=(peers2[d - 1],), device_id_type=MESH).wait_recv()
        copies3.append(forward(d, source))
    for source in range(16):
        at = (1 - core) * 16 + source
        pltpu.make_async_remote_copy(
            src_ref=whole.at[:, at], dst_ref=whole.at[:, at], send_sem=send3.at[0], recv_sem=recv3.at[source],
            device_id=(other,), device_id_type=MESH).wait_recv()

    def pick(p):
        spot, slot = wanted[p]
        rows = whole[p].reshape(256, 128)
        parts = jnp.concatenate(split_three(rows), axis=1)
        wide = lax.broadcasted_iota(jnp.int32, (128, 256), 1)
        take = jnp.where(wide == jnp.concatenate([spot, spot], axis=1), 1.0, 0.0).astype(BF16)
        got = jnp.dot(take, parts, preferred_element_type=F32)
        got = got[:, 0:128] + (got[:, 128:256] + got[:, 256:384])
        got = jnp.where(slot > 0.5, pltpu.roll(got, 64, 1), got)
        return jnp.where(lanes2 < 64, got, 0.0)

    later = prepare(pick, matrix, pivots_t)
    sums = factorise(features_ref, amp_ref, matrix, pivots_t, kern, cross, done, squares, inverse_t,
                     (None, upper1, upper2, upper3), raw_first, raw_near, raw_far, factor_ref, later)

    lane8 = lax.broadcasted_iota(jnp.int32, (8, 128), 1)
    own_squares = amp_ref[...] * amp_ref[...]
    total = tree([own_squares[8 * b:8 * b + 8, :] for b in range(4)])
    value = jnp.zeros((8, 128), F32)
    for p in range(4):
        total = total - sums[p]
        value = jnp.where(lane8 == p, jnp.sum(jnp.sum(total, axis=0, keepdims=True), axis=1, keepdims=True), value)

    my_sums[...] = value[0:1, :]
    all_sums[me] = my_sums[...]
    high, wide = plane // 4, lax.rem(plane, 4)
    targets = []
    for dy, dx, dz, dc in FAR_FIRST:
        there = lax.rem(high + dy, 4) * 4 + lax.rem(wide + dx, 4)
        targets.append(device_of(there, lax.rem(deep + dz, 8), lax.rem(core + dc, 2)))
    for target in targets:
        pltpu.make_async_remote_copy(
            src_ref=my_sums, dst_ref=all_sums.at[me], send_sem=total_sems.at[0], recv_sem=total_sems.at[1],
            device_id=(target,), device_id_type=MESH).start()
    every = pltpu.make_async_remote_copy(
        src_ref=all_sums.at[0:255], dst_ref=all_sums.at[0:255], send_sem=total_sems.at[0], recv_sem=total_sems.at[1],
        device_id=(targets[0],), device_id_type=MESH)
    residuals(amp_ref, squares, factor_ref, residual_ref)
    every.wait_recv()
    means_ref[...] = jnp.sum(all_sums[...], axis=0)[:, 0:4] * (1.0 / points)
    every.wait_send()
    for copy in copies1 + copies2 + copies3:
        copy.wait_send()


def write_kernel(factor_ref, residual_ref, means_ref, factor_hbm, residual_hbm, means_hbm, sems):
    copies = [
        pltpu.make_async_copy(residual_ref, residual_hbm, sems.at[8]),
        pltpu.make_async_copy(means_ref, means_hbm, sems.at[9]),
    ]
    for part in range(8):
        rows = pl.ds(512 * part, 512)
        copies.append(pltpu.make_async_copy(factor_ref.at[rows], factor_hbm.at[rows], sems.at[part]))
    for copy in copies:
        copy.start()
    for copy in copies:
        copy.wait()


def local(embed, amplitude, pivots):
    points = 4096 * lax.axis_size("rows")
    operands = [
        pltpu.with_memory_space_constraint(value, pltpu.HBM)
        for value in (pivots, embed.T, amplitude.reshape(32, 128))
    ]
    factor, residual, means = pl.pallas_call(
        functools.partial(whole_kernel, points),
        out_shape=(jax.ShapeDtypeStruct((4096, 512), F32), jax.ShapeDtypeStruct((32, 128), F32),
                   jax.ShapeDtypeStruct((1, 4), F32)),
        in_specs=[pl.BlockSpec(memory_space=pltpu.HBM)] * 3,
        out_specs=[pl.BlockSpec(memory_space=pltpu.VMEM)] * 3,
        scratch_shapes=[
            pltpu.VMEM((4, 128), jnp.int32), pltpu.VMEM((64, 4096), F32), pltpu.VMEM((32, 128), F32),
            pltpu.SemaphoreType.DMA((3,)),
            pltpu.VMEM((4096, 256), BF16),
            pltpu.VMEM((4, 128), F32), pltpu.VMEM((8, 4, 128), F32), pltpu.VMEM((4, 32, 8, 128), F32),
            pltpu.SemaphoreType.DMA((7,)), pltpu.SemaphoreType.DMA((8,)),
            pltpu.SemaphoreType.DMA((15,)), pltpu.SemaphoreType.DMA((16,)),
            pltpu.SemaphoreType.DMA((16,)), pltpu.SemaphoreType.DMA((16,)),
            pltpu.VMEM((1, 128), F32), pltpu.VMEM((256, 1, 128), F32), pltpu.SemaphoreType.DMA((2,)),
        ] + SCRATCH,
        compiler_params=pltpu.CompilerParams(collective_id=0, has_side_effects=True, vmem_limit_bytes=45000000),
        name="pivoted_cholesky",
    )(*operands)
    factor, residual, means = pl.pallas_call(
        write_kernel,
        out_shape=(jax.ShapeDtypeStruct((4096, 512), F32), jax.ShapeDtypeStruct((32, 128), F32),
                   jax.ShapeDtypeStruct((1, 4), F32)),
        in_specs=[pl.BlockSpec(memory_space=pltpu.VMEM)] * 3,
        out_specs=[pl.BlockSpec(memory_space=pltpu.HBM)] * 3,
        scratch_shapes=[pltpu.SemaphoreType.DMA((10,))],
        compiler_params=pltpu.CompilerParams(vmem_limit_bytes=1 << 20),
        name="write_out",
    )(factor, residual, means)
    return factor, residual.reshape(4096), means.reshape(4)


def solution(mesh):
    return jax.shard_map(
        local,
        mesh=mesh,
        in_specs=(P("rows", None), P("rows"), P()),
        out_specs=(P("rows", None), P("rows"), P()),
        check_vma=False,
    )
```
